256 devices in a mesh: dp: 8 (over x, core), clus: 32 (over z, y).
Axes of the slice: x: 4, y: 4, z: 8, core: 2. Of those that a mesh axis runs over, the one named last changes fastest.
Arguments:
- activations: bfloat16 [1024, 12288], P('clus', 'dp'), may hold values from -6 to 6
- picks: int32 [1024, 48], replicated, may hold values from 0 to 383, all different within a row
- up_weight: bfloat16 [384, 12288, 128], P('clus', 'dp'), may hold values from -0.0546875 to 0.0546875
- up_bias: float32 [384, 128], P('clus'), may hold values from -3 to 3
- down_weight: bfloat16 [384, 128, 12288], P('clus', None, 'dp'), may hold values from -0.078125 to 0.078125
Outputs:
- layer_out: bfloat16 [1024, 12288], P('clus', 'dp')
The draws below stay inside these ranges and needn't reach their ends.
Inputs may be any that keep to these rules, and one draw needn't show every extreme that they name: `picks`: each row names 48 distinct clusters; every cluster is named by some row.
All inputs are finite; a program needn't handle non-finite values.
Results may differ from the reference program's by a relative error of at most 0.012.
Values may be sent and summed in bfloat16 or wider, within the bound.
No kernel may reach another device: no remote copies, remote signals or barrier semaphores. Data moves between devices by JAX's collectives and lax.ppermute only.
A program may use at most 64 MiB of HBM per device.

```python
import jax
import jax.numpy as jnp
from jax import lax

D = 12288
NEUR = 128
CL_DEV = 12
TOP = 48
NCLUS = 384
TOKENS = 1024


def block_levels(own_key, dims, shards, low, high):
    def one(axis_at, blocks):
        steps = jax.random.uniform(jax.random.fold_in(jax.random.fold_in(own_key, 6), axis_at), (blocks,), jnp.float32, low / len(shards), high / len(shards))
        return jnp.repeat(jnp.exp(steps), dims[axis_at] // blocks).reshape((-1,) + (1,) * (len(dims) - axis_at - 1))

    loudness = one(*shards[0])
    for cut in shards[1:]:
        loudness = loudness * one(*cut)
    return loudness


def distinct(key, rows, count, top, lift):
    ranking = jax.random.permutation(jax.random.fold_in(key, 1), count)
    boost = ranking
    for power in range(3):
        boost = boost * boost // count
    boost = boost * lift // count
    lots = jax.random.randint(jax.random.fold_in(key, 2), (rows, count), 0, 4096) + boost
    holders = jax.random.permutation(jax.random.fold_in(key, 3), rows)[jnp.arange(count) % rows]
    lots = jnp.where(jnp.arange(rows)[:, None] == holders[None, :], 1 << 14, lots)
    priority = lots * count + jnp.arange(count)
    return lax.top_k(priority.astype(jnp.int32), top)[1].astype(jnp.int32)


def noise(own_key, extent, width, reach, split=(), kind=jnp.bfloat16):
    entries = jax.random.normal(own_key, extent, jnp.float32) * width
    if len(split) > 0:
        entries = block_levels(own_key, extent, split, -0.22, 0.18) * entries
    return jnp.clip(entries, min=-reach, max=reach).astype(kind)


def setup_inputs(seed: int = 0) -> dict:
    key_of = jax.random.split(jax.random.key(seed), 6)
    activations = noise(key_of[0], (TOKENS, D), 1.0, 6.0, ((0, 32), (1, 8)))
    picks = distinct(key_of[1], TOKENS, NCLUS, TOP, 1024)
    up_weight = noise(key_of[2], (NCLUS, D, NEUR), D ** -0.5, 0.0546875, ((0, 32), (1, 8)))
    up_bias = noise(key_of[3], (NCLUS, NEUR), 0.5, 3.0, ((0, 32),), jnp.float32)
    down_weight = noise(key_of[4], (NCLUS, NEUR, D), (TOP * NEUR) ** -0.5, 0.078125, ((0, 32), (2, 8)))
    return {"activations": activations, "picks": picks, "up_weight": up_weight, "up_bias": up_bias, "down_weight": down_weight}


def reference(activations, picks, up_weight, up_bias, down_weight):
    ngroups = NCLUS // CL_DEV
    features = activations.shape[1]
    columns = jnp.arange(CL_DEV, dtype=jnp.int32)

    def one_group(running, group_index):
        start = (group_index * CL_DEV).astype(jnp.int32)
        wanted = start + columns
        cluster_mask = jnp.any(picks[:, :, None] == wanted[None, None, :], axis=1).astype(jnp.float32)
        up_block = lax.dynamic_slice_in_dim(up_weight, start, CL_DEV, 0)
        up_block = jnp.transpose(up_block, (1, 0, 2)).reshape(features, CL_DEV * NEUR)
        preact = jnp.dot(activations, up_block, preferred_element_type=jnp.float32).reshape(TOKENS, CL_DEV, NEUR)
        bias_block = lax.dynamic_slice_in_dim(up_bias, start, CL_DEV, 0)
        hidden = (jnp.maximum(preact + bias_block[None], 0.0) * cluster_mask[:, :, None]).astype(jnp.bfloat16)
        down_block = lax.dynamic_slice_in_dim(down_weight, start, CL_DEV, 0).reshape(CL_DEV * NEUR, features)
        partial_value = jnp.dot(hidden.reshape(TOKENS, CL_DEV * NEUR), down_block,
                          preferred_element_type=jnp.float32).astype(jnp.bfloat16)
        partial_value = lax.optimization_barrier(partial_value)
        return running + partial_value.astype(jnp.float32), None

    running, unused = lax.scan(one_group, jnp.zeros((TOKENS, features), jnp.float32),
                               jnp.arange(ngroups, dtype=jnp.int32))
    return running.astype(jnp.bfloat16)
```

```python
import jax
import jax.numpy as jnp
from jax import lax
from jax.sharding import Mesh
from jax.sharding import PartitionSpec as P

F32, BF16 = jnp.float32, jnp.bfloat16


def spread(block, axis):
    peers = lax.axis_size(axis)
    return lax.all_to_all(
        jnp.broadcast_to(block[None], (peers,) + block.shape), axis, split_axis=0, concat_axis=0
    )


def exchange(blocks, axis):
    return lax.all_to_all(blocks, axis, split_axis=0, concat_axis=0)


def total(blocks):
    return jnp.sum(blocks.astype(F32), axis=0)


def swap(block):
    return lax.ppermute(block, "core", [(0, 1), (1, 0)])


def on_device(activations, picks, up_weight, up_bias, down_weight):
    nx, nz, ny = lax.axis_size("x"), lax.axis_size("z"), lax.axis_size("y")
    rows, width = activations.shape
    clusters, _, neurons = up_weight.shape
    tokens = nz * ny * rows
    cut = width // 2
    half = clusters // 2
    core, xi = lax.axis_index("core"), lax.axis_index("x")
    group = lax.axis_index("z") * ny + lax.axis_index("y")

    second = spread(activations[:, cut:], "y")
    first, second = lax.optimization_barrier((activations[:, :cut], second))
    x_b = lax.all_gather(second, "z", axis=0).reshape(tokens, -1)
    x_a = spread(spread(first, "z"), "y")
    x_a = jnp.transpose(x_a, (1, 0, 2, 3)).reshape(tokens, cut)

    def up(start):
        w = lax.dynamic_slice_in_dim(up_weight, start, half, 0)
        part = jnp.einsum("td,cdn->ctn", x_a, w[:, :cut], preferred_element_type=F32)
        return part + jnp.einsum("td,cdn->ctn", x_b, w[:, cut:], preferred_element_type=F32)

    mine, theirs = core * half, (1 - core) * half
    away = up(theirs).astype(BF16)
    here = up(mine)
    partial = (here + swap(away).astype(F32)).astype(BF16)
    partial = partial.reshape(half, nx, tokens // nx, neurons).transpose(1, 0, 2, 3)
    summed = total(exchange(partial, "x"))

    span = tokens // nx
    picked = lax.dynamic_slice_in_dim(picks, xi * span, span, 0)
    wanted = group * clusters + mine + jnp.arange(half, dtype=jnp.int32)
    mask = jnp.any(picked[None, :, :] == wanted[:, None, None], axis=-1).astype(F32)
    bias = lax.dynamic_slice_in_dim(up_bias, mine, half, 0)
    hidden = (jnp.maximum(summed + bias[:, None, :], 0.0) * mask[:, :, None]).astype(BF16)
    hidden = spread(hidden, "x")
    hidden = hidden.transpose(1, 0, 2, 3).reshape(half, tokens, neurons)
    other = swap(hidden)

    def down(low, high):
        w1 = lax.dynamic_slice_in_dim(down_weight[:, :, low:high], mine, half, 0)
        w2 = lax.dynamic_slice_in_dim(down_weight[:, :, low:high], theirs, half, 0)
        out = jnp.einsum("ctn,cnd->td", hidden, w1, preferred_element_type=F32)
        out = out + jnp.einsum("ctn,cnd->td", other, w2, preferred_element_type=F32)
        return out.astype(BF16)

    out_b = down(cut, width)
    scattered = lax.psum_scatter(out_b, "z", scatter_dimension=0, tiled=True)
    out_a = down(0, cut).reshape(nz, ny, rows, cut).transpose(1, 0, 2, 3)
    out_a = total(exchange(out_a, "y")).astype(BF16)
    out_a = total(exchange(out_a, "z")).astype(BF16)
    out_b = total(exchange(scattered.reshape(ny, rows, -1), "y")).astype(BF16)
    return jnp.concatenate([out_a, out_b], axis=1)


def solution(mesh):
    grid = Mesh(mesh.devices.reshape(4, 2, 8, 4), ("x", "core", "z", "y"))
    dp, clus = ("x", "core"), ("z", "y")
    placed = (P(clus, dp), P(), P(clus, dp, None), P(clus, None), P(clus, None, dp))
    return jax.shard_map(
        on_device, mesh=grid, in_specs=placed, out_specs=P(clus, dp), check_vma=False
    )
```

```python
import functools

import jax
import jax.numpy as jnp
from jax import lax
from jax.experimental import pallas as pl
from jax.experimental.pallas import tpu as pltpu
from jax.sharding import Mesh
from jax.sharding import PartitionSpec as P

F32, BF16, I32 = jnp.float32, jnp.bfloat16, jnp.int32
NX, NC, NZ, NY = 4, 2, 8, 4
SLOTS = 384
TILE = 256


def spread(block, axis):
    peers = lax.axis_size(axis)
    return lax.all_to_all(
        jnp.broadcast_to(block[None], (peers,) + block.shape), axis, split_axis=0, concat_axis=0
    )


def exchange(blocks, axis):
    return lax.all_to_all(blocks, axis, split_axis=0, concat_axis=0)


def total(blocks):
    return jnp.sum(blocks.astype(F32), axis=0)


def from_peer(block, axis, step):
    n = lax.axis_size(axis)
    return lax.ppermute(block, axis, [((i + step) % n, i) for i in range(n)])


def up_kernel(at_ref, xa_ref, xb_ref, w_ref, bias_ref, pos_ref, out_ref, xs, w2, acc):
    cut = xa_ref.shape[-1]
    rows = xa_ref.shape[-2]
    blocks = acc.shape[0]
    span = xs.shape[0] // blocks
    neurons = w_ref.shape[-1]

    @pl.when(pl.program_id(0) == 0)
    def _():
        for z in range(NZ):
            for y in range(NY):
                xs[(z * NY + y) * rows : (z * NY + y + 1) * rows, :cut] = xa_ref[y, z]
                to = (z * NY + lax.rem(at_ref[blocks] + y, NY)) * rows
                xs[pl.ds(pl.multiple_of(to, rows), rows), cut:] = xb_ref[z, y]
        acc[...] = jnp.zeros_like(acc)

    w2[:, :neurons] = w_ref[0]
    w2[:, neurons:] = w_ref[1]
    bias = jnp.concatenate([bias_ref[0, :1], bias_ref[0, 1:]], axis=1)
    slot = lax.broadcasted_iota(I32, (SLOTS, span), 0)

    @pl.loop(0, xs.shape[0] // TILE)
    def _(m):
        pre = jnp.dot(
            xs[pl.ds(pl.multiple_of(m * TILE, TILE), TILE)], w2[...], preferred_element_type=F32
        )
        pre = (pre + bias).astype(BF16)
        for h in range(TILE // span):
            b = m * (TILE // span) + h
            part = pre[h * span : (h + 1) * span]
            both = jnp.concatenate([part[:, :neurons], part[:, neurons:]], axis=0)
            take = jnp.concatenate(
                [
                    jnp.where(slot == pos_ref[0, pl.ds(b, 1), :], 1.0, 0.0),
                    jnp.where(slot == pos_ref[0, pl.ds(blocks + b, 1), :], 1.0, 0.0),
                ],
                axis=1,
            ).astype(BF16)
            acc[b] += jnp.dot(take, both, preferred_element_type=F32)

    @pl.when(pl.program_id(0) == pl.num_programs(0) - 1)
    def _():
        for j in range(blocks):
            out_ref[j] = acc[at_ref[j]].astype(BF16)


def packed_up(at, x_a, x_b, up_weight, bias, pos):
    clusters, width, neurons = up_weight.shape
    tokens = x_a.shape[0] * x_a.shape[1] * x_a.shape[2]
    blocks = NX * NC
    whole = lambda *shape: pl.BlockSpec(shape, lambda i, at: (0,) * len(shape))
    return pl.pallas_call(
        up_kernel,
        grid_spec=pltpu.PrefetchScalarGridSpec(
            num_scalar_prefetch=1,
            grid=(clusters // 2,),
            in_specs=[
                whole(*x_a.shape),
                whole(*x_b.shape),
                pl.BlockSpec((2, width, neurons), lambda i, at: (i, 0, 0)),
                pl.BlockSpec((1, 2, neurons), lambda i, at: (i, 0, 0)),
                pl.BlockSpec((1, 2 * blocks, tokens // blocks), lambda i, at: (i, 0, 0)),
            ],
            out_specs=whole(blocks, SLOTS, neurons),
            scratch_shapes=[
                pltpu.VMEM((tokens, width), BF16),
                pltpu.VMEM((width, 2 * neurons), BF16),
                pltpu.VMEM((blocks, SLOTS, neurons), F32),
            ],
        ),
        out_shape=jax.ShapeDtypeStruct((blocks, SLOTS, neurons), BF16),
        compiler_params=pltpu.CompilerParams(vmem_limit_bytes=32 << 20),
        cost_estimate=pl.CostEstimate(
            flops=2 * tokens * width * clusters * neurons, bytes_accessed=9 << 20, transcendentals=0
        ),
    )(at, x_a, x_b, up_weight, bias, pos)


def unpack_kernel(at_ref, packed_ref, pos_ref, out_ref):
    span, clusters = pos_ref.shape[1:]
    neurons = packed_ref.shape[-1]
    slot = lax.broadcasted_iota(I32, (span, SLOTS), 1)
    for c in range(0, clusters, 2):
        take = jnp.concatenate(
            [jnp.where(slot == pos_ref[0, :, k : k + 1], 1.0, 0.0) for k in (c, c + 1)], axis=0
        ).astype(BF16)
        both = jnp.dot(take, packed_ref[0], preferred_element_type=F32).astype(BF16)
        out_ref[:, c * neurons : (c + 1) * neurons] = both[:span]
        out_ref[:, (c + 1) * neurons : (c + 2) * neurons] = both[span:]


def unpack(at, packed, pos):
    blocks, span, clusters = pos.shape
    neurons = packed.shape[-1]
    return pl.pallas_call(
        unpack_kernel,
        grid_spec=pltpu.PrefetchScalarGridSpec(
            num_scalar_prefetch=1,
            grid=(blocks,),
            in_specs=[
                pl.BlockSpec((1, SLOTS, neurons), lambda j, at: (j, 0, 0)),
                pl.BlockSpec((1, span, clusters), lambda j, at: (at[j], 0, 0)),
            ],
            out_specs=pl.BlockSpec((span, clusters * neurons), lambda j, at: (at[j], 0)),
        ),
        out_shape=jax.ShapeDtypeStruct((blocks * span, clusters * neurons), BF16),
        compiler_params=pltpu.CompilerParams(vmem_limit_bytes=16 << 20),
        cost_estimate=pl.CostEstimate(
            flops=2 * blocks * span * SLOTS * clusters * neurons, bytes_accessed=4 << 20, transcendentals=0
        ),
    )(at, packed, pos)


def down_kernel(y_first, at_ref, hidden_ref, w_ref, out_ref):
    rows = out_ref.shape[-2]
    span = rows * NY
    wide = w_ref[...].reshape(-1, w_ref.shape[-1])

    @pl.loop(0, hidden_ref.shape[0] // TILE)
    def _(m):
        val = jnp.dot(
            hidden_ref[pl.ds(pl.multiple_of(m * TILE, TILE), TILE)], wide, preferred_element_type=F32
        ).astype(BF16)
        for h in range(TILE // span):
            z = m * (TILE // span) + h
            for y in range(NY):
                piece = val[h * span + y * rows : h * span + (y + 1) * rows]
                if y_first:
                    out_ref[y, z] = piece
                else:
                    out_ref[z, lax.rem(y + NY - at_ref[NX * NC], NY)] = piece


def down(at, hidden, down_weight, low, high, y_first):
    tokens, inner = hidden.shape
    clusters, neurons, _ = down_weight.shape
    rows = tokens // (NY * NZ)
    lead = (NY, NZ) if y_first else (NZ, NY)
    return pl.pallas_call(
        functools.partial(down_kernel, y_first),
        grid_spec=pltpu.PrefetchScalarGridSpec(
            num_scalar_prefetch=1,
            grid=((high - low) // TILE,),
            in_specs=[
                pl.BlockSpec((tokens, inner), lambda n, at: (0, 0)),
                pl.BlockSpec((clusters, neurons, TILE), lambda n, at: (0, 0, n + low // TILE)),
            ],
            out_specs=pl.BlockSpec(lead + (rows, TILE), lambda n, at: (0, 0, 0, n)),
        ),
        out_shape=jax.ShapeDtypeStruct(lead + (rows, high - low), BF16),
        compiler_params=pltpu.CompilerParams(vmem_limit_bytes=32 << 20),
        cost_estimate=pl.CostEstimate(
            flops=2 * tokens * inner * (high - low), bytes_accessed=7 << 20, transcendentals=0
        ),
    )(at, hidden, down_weight)


def on_device(activations, picks, up_weight, up_bias, down_weight):
    rows, width = activations.shape
    clusters, _, neurons = up_weight.shape
    tokens = NZ * NY * rows
    blocks = NX * NC
    span = tokens // blocks
    cut = width // 2
    core, xi = lax.axis_index("core"), lax.axis_index("x")
    zi, yi = lax.axis_index("z"), lax.axis_index("y")

    first, second = activations[:, :cut], activations[:, cut:]
    near = jnp.stack([second] + [from_peer(second, "y", k) for k in range(1, NY)])
    x_b = lax.all_gather(near, "z", axis=0)
    x_a = spread(spread(first, "z"), "y")

    wanted = (zi * NY + yi) * clusters + jnp.arange(clusters, dtype=I32)
    mask = jnp.any(picks[:, :, None] == wanted[None, None, :], axis=1)
    hits = mask.reshape(blocks, span, clusters).astype(BF16)
    before = jnp.tril(jnp.ones((span, span), BF16), -1)
    ahead = jnp.triu(jnp.ones((clusters, clusters), BF16), 1)
    each = jnp.sum(hits, axis=2).astype(BF16)
    base = jnp.einsum("bt,st->bs", each, before, preferred_element_type=F32)
    within = jnp.einsum("btk,kc->btc", hits, ahead, preferred_element_type=F32)
    pos = jnp.where(hits > 0, base[:, :, None] + within, -1.0).astype(I32)
    groups = picks.reshape(blocks, span, -1) // clusters
    load = jnp.sum(
        (groups[:, :, :, None] == jnp.arange(NZ * NY, dtype=I32)).astype(I32), axis=(1, 2)
    )
    fits = jnp.max(load) <= SLOTS

    order = [((core + j // NX) % NC) * NX + (xi + j % NX) % NX for j in range(blocks)]
    at = jnp.stack([*order, yi]).astype(I32)

    def packed(x_a, x_b, pos):
        by_pair = pos.transpose(2, 0, 1).reshape(clusters // 2, 2 * blocks, span)
        bias = (up_bias * (1.0 / blocks)).reshape(clusters // 2, 2, neurons)
        part = packed_up(at, x_a, x_b, up_weight, bias, by_pair)
        part = part[:NX].astype(F32) + from_peer(part[NX:], "core", 1).astype(F32)
        summed = part[0]
        part = part.astype(BF16)
        for k in range(1, NX):
            summed = summed + from_peer(part[k], "x", -k).astype(F32)
        own = jnp.maximum(summed, 0.0).astype(BF16)
        own = jnp.stack([own] + [from_peer(own, "x", k) for k in range(1, NX)])
        both = jnp.concatenate([own, from_peer(own, "core", 1)], axis=0)
        return unpack(at, both, pos)

    def dense(x_a, x_b, pos):
        x_0 = x_a.transpose(1, 0, 2, 3).reshape(tokens, cut)
        x_1 = jnp.roll(x_b, yi, axis=1).reshape(tokens, width - cut)
        part = jnp.einsum("td,cdn->tcn", x_0, up_weight[:, :cut], preferred_element_type=F32)
        part += jnp.einsum("td,cdn->tcn", x_1, up_weight[:, cut:], preferred_element_type=F32)
        part = part.astype(BF16).reshape(blocks, span, clusters, neurons)
        summed = total(exchange(part, ("x", "core"))) + up_bias[None]
        keep = lax.dynamic_index_in_dim(pos, xi * NC + core, 0, keepdims=False) >= 0
        own = jnp.where(keep[:, :, None], jnp.maximum(summed, 0.0), 0.0).astype(BF16)
        return spread(own, ("x", "core")).reshape(tokens, clusters * neurons)

    hidden = lax.cond(fits, packed, dense, x_a, x_b, pos)

    out_b = down(at, hidden, down_weight, cut, width, False)
    out_b = lax.psum_scatter(out_b, "z", scatter_dimension=0)
    out_a = down(at, hidden, down_weight, 0, cut, True)
    out_a = total(exchange(out_a, "y")).astype(BF16)
    out_a = total(exchange(out_a, "z")).astype(BF16)
    done = out_b[0].astype(F32)
    for k in range(1, NY):
        done = done + from_peer(out_b[k], "y", -k).astype(F32)
    return jnp.concatenate([out_a, done.astype(BF16)], axis=1)


def solution(mesh):
    grid = Mesh(mesh.devices.reshape(NX, NC, NZ, NY), ("x", "core", "z", "y"))
    dp, clus = ("x", "core"), ("z", "y")
    placed = (P(clus, dp), P(), P(clus, dp, None), P(clus, None), P(clus, None, dp))
    return jax.shard_map(
        on_device, mesh=grid, in_specs=placed, out_specs=P(clus, dp), check_vma=False
    )
```

```python
import functools

import jax
import jax.numpy as jnp
from jax import lax
from jax.experimental import pallas as pl
from jax.experimental.pallas import tpu as pltpu
from jax.sharding import Mesh
from jax.sharding import PartitionSpec as P

F32, BF16, I32 = jnp.float32, jnp.bfloat16, jnp.int32
NX, NC, NZ, NY = 4, 2, 8, 4
BLOCKS = NX * NC
SLOTS = 192
PACK = 4
TILE = 512
VMEM = 32 << 20


def spread(block, axis):
    peers = lax.axis_size(axis)
    return lax.all_to_all(
        jnp.broadcast_to(block[None], (peers,) + block.shape), axis, split_axis=0, concat_axis=0
    )


def exchange(blocks, axis):
    return lax.all_to_all(blocks, axis, split_axis=0, concat_axis=0)


def total(blocks):
    return jnp.sum(blocks.astype(F32), axis=0)


def from_peer(block, axis, step):
    n = lax.axis_size(axis)
    return lax.ppermute(block, axis, [((i + step) % n, i) for i in range(n)])


def up_kernel(at_ref, x_ref, w_ref, bias_ref, pos_ref, out_ref, acc):
    span, neurons = x_ref.shape[0] // BLOCKS, w_ref.shape[-1]
    slot = lax.broadcasted_iota(I32, (SLOTS, PACK * span), 0)

    @pl.when(pl.program_id(0) == 0)
    def _():
        acc[...] = jnp.zeros_like(acc)

    pairs = []
    for p in range(0, PACK, 2):
        wide = jnp.concatenate([w_ref[p], w_ref[p + 1]], axis=1)
        bias = jnp.concatenate([bias_ref[0, p : p + 1], bias_ref[0, p + 1 : p + 2]], axis=1)
        pre = jnp.dot(x_ref[...], wide, preferred_element_type=F32)
        pairs.append((pre + bias).astype(BF16))
    for b in range(BLOCKS):
        rows = slice(b * span, (b + 1) * span)
        both = jnp.concatenate(
            [p[rows, k * neurons : (k + 1) * neurons] for p in pairs for k in range(2)], axis=0
        )
        take = jnp.where(slot == pos_ref[0, b : b + 1, :], 1.0, 0.0).astype(BF16)
        acc[b] += jnp.dot(take, both, preferred_element_type=F32)

    @pl.when(pl.program_id(0) == pl.num_programs(0) - 1)
    def _():
        for j in range(BLOCKS):
            out_ref[j] = acc[at_ref[j]].astype(BF16)


def packed_up(at, x, up_weight, bias, pos):
    clusters, width, neurons = up_weight.shape
    tokens = x.shape[0]
    return pl.pallas_call(
        up_kernel,
        grid_spec=pltpu.PrefetchScalarGridSpec(
            num_scalar_prefetch=1,
            grid=(clusters // PACK,),
            in_specs=[
                pl.BlockSpec((tokens, width), lambda i, at: (0, 0)),
                pl.BlockSpec((PACK, width, neurons), lambda i, at: (i, 0, 0)),
                pl.BlockSpec((1, PACK, neurons), lambda i, at: (i, 0, 0)),
                pl.BlockSpec((1, BLOCKS, PACK * tokens // BLOCKS), lambda i, at: (i, 0, 0)),
            ],
            out_specs=pl.BlockSpec((BLOCKS, SLOTS, neurons), lambda i, at: (0, 0, 0)),
            scratch_shapes=[pltpu.VMEM((BLOCKS, SLOTS, neurons), F32)],
        ),
        out_shape=jax.ShapeDtypeStruct((BLOCKS, SLOTS, neurons), BF16),
        compiler_params=pltpu.CompilerParams(vmem_limit_bytes=VMEM),
        cost_estimate=pl.CostEstimate(
            flops=2 * tokens * width * clusters * neurons, bytes_accessed=7 << 20, transcendentals=0
        ),
    )(at, x, up_weight, bias, pos)


def down_kernel(y_first, at_ref, packed_ref, pos_ref, w_ref, out_ref, hidden):
    neurons = packed_ref.shape[-1]
    span = hidden.shape[0] // BLOCKS
    rows = out_ref.shape[-2]

    @pl.when(pl.program_id(0) == 0)
    def _():
        slot = lax.broadcasted_iota(I32, (SLOTS, PACK * span), 0)
        for j in range(BLOCKS):
            b = at_ref[j]
            to = pl.ds(pl.multiple_of(b * span, span), span)
            for q in range(pos_ref.shape[0]):
                take = jnp.where(slot == pos_ref[q, pl.ds(b, 1), :], 1.0, 0.0).astype(BF16)
                both = lax.dot_general(
                    take, packed_ref[j], (((0,), (0,)), ((), ())), preferred_element_type=F32
                ).astype(BF16)
                for k in range(PACK):
                    c = q * PACK + k
                    hidden[to, c * neurons : (c + 1) * neurons] = both[k * span : (k + 1) * span]

    wide = w_ref[...].reshape(-1, w_ref.shape[-1])
    val = jnp.dot(hidden[...], wide, preferred_element_type=F32).astype(BF16)
    for y in range(NY):
        for z in range(NZ):
            if y_first:
                out_ref[y, z] = val[(z * NY + y) * rows : (z * NY + y + 1) * rows]
            else:
                out_ref[z, y] = val[(y * NZ + z) * rows : (y * NZ + z + 1) * rows]


def packed_down(at, packed, pos, down_weight, tokens, y_first):
    clusters, neurons, width = down_weight.shape
    rows = tokens // (NY * NZ)
    lead = (NY, NZ) if y_first else (NZ, NY)
    return pl.pallas_call(
        functools.partial(down_kernel, y_first),
        grid_spec=pltpu.PrefetchScalarGridSpec(
            num_scalar_prefetch=1,
            grid=(width // TILE,),
            in_specs=[
                pl.BlockSpec(packed.shape, lambda n, at: (0, 0, 0)),
                pl.BlockSpec(pos.shape, lambda n, at: (0, 0, 0)),
                pl.BlockSpec((clusters, neurons, TILE), lambda n, at: (0, 0, n)),
            ],
            out_specs=pl.BlockSpec(lead + (rows, TILE), lambda n, at: (0, 0, 0, n)),
            scratch_shapes=[pltpu.VMEM((tokens, clusters * neurons), BF16)],
        ),
        out_shape=jax.ShapeDtypeStruct(lead + (rows, width), BF16),
        compiler_params=pltpu.CompilerParams(vmem_limit_bytes=VMEM),
        cost_estimate=pl.CostEstimate(
            flops=2 * tokens * clusters * neurons * width, bytes_accessed=7 << 20, transcendentals=0
        ),
    )(at, packed, pos, down_weight)


def slots_of(mask):
    clusters, _, span = mask.shape
    hits = mask.astype(BF16)
    before = jnp.triu(jnp.ones((span, span), BF16), 1)
    ahead = jnp.triu(jnp.ones((clusters, clusters), BF16), 1)
    each = jnp.sum(hits.astype(F32), axis=0).astype(BF16)
    base = jnp.dot(each, before, preferred_element_type=F32)
    within = jnp.einsum("kbt,kc->cbt", hits, ahead, preferred_element_type=F32)
    return jnp.where(mask, base[None] + within, -1.0).astype(I32)


def dense(activations, picks, up_weight, up_bias, down_weight):
    rows, width = activations.shape
    clusters, _, neurons = up_weight.shape
    tokens, span = picks.shape[0], picks.shape[0] // BLOCKS
    x = spread(spread(activations, "y"), "z").reshape(tokens, width)
    part = jnp.einsum("td,cdn->tcn", x, up_weight, preferred_element_type=F32).astype(BF16)
    part = part.reshape(BLOCKS, span, clusters, neurons)
    summed = total(exchange(part, ("x", "core"))) + up_bias[None]
    at = lax.axis_index("x") * NC + lax.axis_index("core")
    group = lax.axis_index("z") * NY + lax.axis_index("y")
    picked = lax.dynamic_slice_in_dim(picks, at * span, span, 0)
    wanted = group * clusters + jnp.arange(clusters, dtype=I32)
    keep = jnp.any(picked[:, :, None] == wanted[None, None, :], axis=1)
    hidden = jnp.where(keep[:, :, None], jnp.maximum(summed, 0.0), 0.0).astype(BF16)
    hidden = spread(hidden, ("x", "core")).reshape(tokens, clusters, neurons)
    out = jnp.einsum("tcn,cnd->td", hidden, down_weight, preferred_element_type=F32)
    out = exchange(out.astype(BF16).reshape(NZ, NY, rows, width), "z")
    out = exchange(total(out).astype(BF16), "y")
    return total(out).astype(BF16)


def on_device(activations, picks, up_weight, up_bias, down_weight):
    rows, width = activations.shape
    clusters, _, neurons = up_weight.shape
    cut = rows // 2
    tokens = NZ * NY * cut
    span = tokens // BLOCKS
    core, xi = lax.axis_index("core"), lax.axis_index("x")
    zi, yi = lax.axis_index("z"), lax.axis_index("y")

    first, second = activations[:cut], activations[cut:]
    near = jnp.stack([second] + [from_peer(second, "y", k) for k in range(1, NY)])
    near = jnp.roll(near, yi, axis=0)
    near, first = lax.optimization_barrier((near, first))
    x_2 = lax.all_gather(near, "z", axis=0).reshape(tokens, width)
    x_1 = spread(spread(first, "z"), "y").reshape(tokens, width)

    wanted = (zi * NY + yi) * clusters + jnp.arange(clusters, dtype=I32)
    mask = jnp.any(picks.T[None, :, :] == wanted[:, None, None], axis=1)
    mask = mask.reshape(clusters, NZ, NY, 2, cut)
    mask_1 = mask[:, :, :, 0].transpose(0, 2, 1, 3).reshape(clusters, BLOCKS, span)
    mask_2 = mask[:, :, :, 1].reshape(clusters, BLOCKS, span)
    pos = slots_of(jnp.concatenate([mask_1, mask_2], axis=1))
    pos = pos.reshape(clusters // PACK, PACK, 2 * BLOCKS, span).transpose(0, 2, 1, 3)
    pos = pos.reshape(clusters // PACK, 2 * BLOCKS, PACK * span)
    pos_1, pos_2 = pos[:, :BLOCKS], pos[:, BLOCKS:]
    groups = picks.T.reshape(-1, NZ, NY, 2, cut) // clusters
    load = jnp.sum(
        (groups[None] == jnp.arange(NZ * NY, dtype=I32)[:, None, None, None, None, None]).astype(I32),
        axis=(1, 5),
    )
    pairs = load[:, :, :, 0].reshape(NZ * NY, BLOCKS // NY, NZ * NY // BLOCKS, NY).sum(axis=2)
    room = jnp.maximum(jnp.max(pairs), jnp.max(load[:, :, :, 1].sum(axis=2)))
    fits = room <= SLOTS

    order = [((core + j // NX) % NC) * NX + (xi + j % NX) % NX for j in range(BLOCKS)]
    at = jnp.stack(order).astype(I32)
    bias = (up_bias * (1.0 / BLOCKS)).reshape(clusters // PACK, PACK, neurons)

    def sum_of(part):
        part = part[:NX].astype(F32) + from_peer(part[NX:], "core", 1).astype(F32)
        summed = part[0]
        part = part.astype(BF16)
        for k in range(1, NX):
            summed = summed + from_peer(part[k], "x", -k).astype(F32)
        return jnp.maximum(summed, 0.0).astype(BF16)

    def all_of(own):
        own = jnp.stack([own] + [from_peer(own, "x", k) for k in range(1, NX)])
        return jnp.concatenate([own, from_peer(own, "core", 1)], axis=0)

    own_1 = sum_of(packed_up(at, x_1, up_weight, bias, pos_1))
    part_2 = packed_up(at, x_2, up_weight, bias, pos_2)
    own_1, part_2 = lax.optimization_barrier((own_1, part_2))
    hidden_1 = all_of(own_1)
    hidden_2 = all_of(sum_of(part_2))
    out_1 = packed_down(at, hidden_1, pos_1, down_weight, tokens, False)
    out_1 = lax.psum_scatter(out_1, "z", scatter_dimension=0)
    out_2 = packed_down(at, hidden_2, pos_2, down_weight, tokens, True)
    out_2 = total(exchange(out_2, "y")).astype(BF16)
    out_2 = total(exchange(out_2, "z")).astype(BF16)
    out_1 = jnp.roll(out_1, -yi, axis=0)
    done = out_1[0].astype(F32)
    for k in range(1, NY):
        done = done + from_peer(out_1[k], "y", -k).astype(F32)
    out = jnp.concatenate([done.astype(BF16), out_2], axis=0)
    whole = (activations, picks, up_weight, up_bias, down_weight)
    return lax.cond(fits, lambda: out, lambda: dense(*whole))


def solution(mesh):
    grid = Mesh(mesh.devices.reshape(NX, NC, NZ, NY), ("x", "core", "z", "y"))
    dp, clus = ("x", "core"), ("z", "y")
    placed = (P(clus, dp), P(), P(clus, dp, None), P(clus, None), P(clus, None, dp))
    return jax.shard_map(
        on_device, mesh=grid, in_specs=placed, out_specs=P(clus, dp), check_vma=False
    )
```

```python
import jax
import jax.numpy as jnp
from jax import lax
from jax.experimental import pallas as pl
from jax.experimental.pallas import tpu as pltpu
from jax.sharding import Mesh
from jax.sharding import PartitionSpec as P

F32, BF16, I32 = jnp.float32, jnp.bfloat16, jnp.int32
NX, NC, NZ, NY = 4, 2, 8, 4
BLOCKS = NX * NC
SLOTS = 192
PACK = 4
TILE = 512
VMEM = 32 << 20


def spread(block, axis):
    peers = lax.axis_size(axis)
    return lax.all_to_all(
        jnp.broadcast_to(block[None], (peers,) + block.shape), axis, split_axis=0, concat_axis=0
    )


def exchange(blocks, axis):
    return lax.all_to_all(blocks, axis, split_axis=0, concat_axis=0)


def total(blocks):
    return jnp.sum(blocks.astype(F32), axis=0)


def from_peer(block, axis, step):
    n = lax.axis_size(axis)
    return lax.ppermute(block, axis, [((i + step) % n, i) for i in range(n)])


def ring_spread(block, axis):
    near = jnp.stack([from_peer(block, axis, -1), block, from_peer(block, axis, 1)])
    ahead = from_peer(near, axis, 3)
    behind = from_peer(near[1:], axis, -3)
    blocks = jnp.concatenate([near[1:], ahead, behind, near[:1]])
    return jnp.roll(blocks, lax.axis_index(axis), axis=0)


def ring_total(blocks, axis):
    blocks = jnp.roll(blocks, -lax.axis_index(axis), axis=0)
    behind = from_peer(blocks[2:5], axis, -3).astype(F32)
    ahead = from_peer(blocks[5:7], axis, 3).astype(F32)
    low = (blocks[7] + behind[0]).astype(BF16)
    high = (blocks[1] + behind[2] + ahead[1]).astype(BF16)
    mine = blocks[0] + behind[1] + ahead[0]
    return mine + from_peer(high, axis, -1).astype(F32) + from_peer(low, axis, 1).astype(F32)


def up_kernel(at_ref, x_ref, w_ref, bias_ref, pos_ref, out_ref, acc):
    span, neurons = x_ref.shape[0] // BLOCKS, w_ref.shape[-1]
    slot = lax.broadcasted_iota(I32, (SLOTS, PACK * span), 0)

    @pl.when(pl.program_id(0) == 0)
    def _():
        acc[...] = jnp.zeros_like(acc)

    pairs = []
    for p in range(0, PACK, 2):
        wide = jnp.concatenate([w_ref[p], w_ref[p + 1]], axis=1)
        bias = jnp.concatenate([bias_ref[0, p : p + 1], bias_ref[0, p + 1 : p + 2]], axis=1)
        pre = jnp.dot(x_ref[...], wide, preferred_element_type=F32)
        pairs.append((pre + bias).astype(BF16))
    for b in range(BLOCKS):
        rows = slice(b * span, (b + 1) * span)
        both = jnp.concatenate(
            [p[rows, k * neurons : (k + 1) * neurons] for p in pairs for k in range(2)], axis=0
        )
        take = jnp.where(slot == pos_ref[0, b : b + 1, :], 1.0, 0.0).astype(BF16)
        acc[b] += jnp.dot(take, both, preferred_element_type=F32)

    @pl.when(pl.program_id(0) == pl.num_programs(0) - 1)
    def _():
        for j in range(BLOCKS):
            out_ref[j] = acc[at_ref[j]].astype(BF16)


def packed_up(at, x, up_weight, bias, pos):
    clusters, width, neurons = up_weight.shape
    tokens = x.shape[0]
    return pl.pallas_call(
        up_kernel,
        grid_spec=pltpu.PrefetchScalarGridSpec(
            num_scalar_prefetch=1,
            grid=(clusters // PACK,),
            in_specs=[
                pl.BlockSpec((tokens, width), lambda i, at: (0, 0)),
                pl.BlockSpec((PACK, width, neurons), lambda i, at: (i, 0, 0)),
                pl.BlockSpec((1, PACK, neurons), lambda i, at: (i, 0, 0)),
                pl.BlockSpec((1, BLOCKS, PACK * tokens // BLOCKS), lambda i, at: (i, 0, 0)),
            ],
            out_specs=pl.BlockSpec((BLOCKS, SLOTS, neurons), lambda i, at: (0, 0, 0)),
            scratch_shapes=[pltpu.VMEM((BLOCKS, SLOTS, neurons), F32)],
        ),
        out_shape=jax.ShapeDtypeStruct((BLOCKS, SLOTS, neurons), BF16),
        compiler_params=pltpu.CompilerParams(vmem_limit_bytes=VMEM),
        cost_estimate=pl.CostEstimate(
            flops=2 * tokens * width * clusters * neurons, bytes_accessed=7 << 20, transcendentals=0
        ),
    )(at, x, up_weight, bias, pos)


def down_kernel(at_ref, packed_ref, pos_ref, w_ref, out_ref, hidden):
    neurons = packed_ref.shape[-1]
    span = hidden.shape[0] // BLOCKS

    @pl.when(pl.program_id(0) == 0)
    def _():
        slot = lax.broadcasted_iota(I32, (SLOTS, PACK * span), 0)
        for j in range(BLOCKS):
            b = at_ref[j]
            to = pl.ds(pl.multiple_of(b * span, span), span)
            for q in range(pos_ref.shape[0]):
                take = jnp.where(slot == pos_ref[q, pl.ds(b, 1), :], 1.0, 0.0).astype(BF16)
                both = lax.dot_general(
                    take, packed_ref[j], (((0,), (0,)), ((), ())), preferred_element_type=F32
                ).astype(BF16)
                for k in range(PACK):
                    c = q * PACK + k
                    hidden[to, c * neurons : (c + 1) * neurons] = both[k * span : (k + 1) * span]

    wide = w_ref[...].reshape(-1, w_ref.shape[-1])
    out_ref[...] = jnp.dot(hidden[...], wide, preferred_element_type=F32).astype(BF16)


def packed_down(at, packed, pos, down_weight, tokens):
    clusters, neurons, width = down_weight.shape
    return pl.pallas_call(
        down_kernel,
        grid_spec=pltpu.PrefetchScalarGridSpec(
            num_scalar_prefetch=1,
            grid=(width // TILE,),
            in_specs=[
                pl.BlockSpec(packed.shape, lambda n, at: (0, 0, 0)),
                pl.BlockSpec(pos.shape, lambda n, at: (0, 0, 0)),
                pl.BlockSpec((clusters, neurons, TILE), lambda n, at: (0, 0, n)),
            ],
            out_specs=pl.BlockSpec((tokens, TILE), lambda n, at: (0, n)),
            scratch_shapes=[pltpu.VMEM((tokens, clusters * neurons), BF16)],
        ),
        out_shape=jax.ShapeDtypeStruct((tokens, width), BF16),
        compiler_params=pltpu.CompilerParams(vmem_limit_bytes=VMEM),
        cost_estimate=pl.CostEstimate(
            flops=2 * tokens * clusters * neurons * width, bytes_accessed=7 << 20, transcendentals=0
        ),
    )(at, packed, pos, down_weight)


def slots_of(mask):
    clusters, _, span = mask.shape
    hits = mask.astype(BF16)
    before = jnp.triu(jnp.ones((span, span), BF16), 1)
    ahead = jnp.triu(jnp.ones((clusters, clusters), BF16), 1)
    each = jnp.sum(hits.astype(F32), axis=0).astype(BF16)
    base = jnp.dot(each, before, preferred_element_type=F32)
    within = jnp.einsum("kbt,kc->cbt", hits, ahead, preferred_element_type=F32)
    return jnp.where(mask, base[None] + within, -1.0).astype(I32)


def dense(activations, picks, up_weight, up_bias, down_weight):
    rows, width = activations.shape
    clusters, _, neurons = up_weight.shape
    tokens, span = picks.shape[0], picks.shape[0] // BLOCKS
    x = spread(spread(activations, "y"), "z").reshape(tokens, width)
    part = jnp.einsum("td,cdn->tcn", x, up_weight, preferred_element_type=F32).astype(BF16)
    part = part.reshape(BLOCKS, span, clusters, neurons)
    summed = total(exchange(part, ("x", "core"))) + up_bias[None]
    at = lax.axis_index("x") * NC + lax.axis_index("core")
    group = lax.axis_index("z") * NY + lax.axis_index("y")
    picked = lax.dynamic_slice_in_dim(picks, at * span, span, 0)
    wanted = group * clusters + jnp.arange(clusters, dtype=I32)
    keep = jnp.any(picked[:, :, None] == wanted[None, None, :], axis=1)
    hidden = jnp.where(keep[:, :, None], jnp.maximum(summed, 0.0), 0.0).astype(BF16)
    hidden = spread(hidden, ("x", "core")).reshape(tokens, clusters, neurons)
    out = jnp.einsum("tcn,cnd->td", hidden, down_weight, preferred_element_type=F32)
    out = exchange(out.astype(BF16).reshape(NZ, NY, rows, width), "z")
    out = exchange(total(out).astype(BF16), "y")
    return total(out).astype(BF16)


def on_device(activations, picks, up_weight, up_bias, down_weight):
    rows, width = activations.shape
    clusters, _, neurons = up_weight.shape
    cut = rows // 2
    tokens = NZ * NY * cut
    span = tokens // BLOCKS
    core, xi = lax.axis_index("core"), lax.axis_index("x")
    zi, yi = lax.axis_index("z"), lax.axis_index("y")

    first = spread(activations[:cut], "z")
    second = activations[cut:]
    x_1 = spread(first, "y")
    second, x_1 = lax.optimization_barrier((ring_spread(second, "z"), x_1))
    x_1 = x_1.reshape(tokens, width)
    x_2 = spread(second, "y").reshape(tokens, width)

    wanted = (zi * NY + yi) * clusters + jnp.arange(clusters, dtype=I32)
    mask = jnp.any(picks.T[None, :, :] == wanted[:, None, None], axis=1)
    mask = mask.reshape(clusters, NZ, NY, 2, cut).transpose(0, 3, 2, 1, 4)
    pos = slots_of(mask.reshape(clusters, 2 * BLOCKS, span))
    pos = pos.reshape(clusters // PACK, PACK, 2 * BLOCKS, span).transpose(0, 2, 1, 3)
    pos = pos.reshape(clusters // PACK, 2 * BLOCKS, PACK * span)
    pos_1, pos_2 = pos[:, :BLOCKS], pos[:, BLOCKS:]

    groups = picks.T // clusters
    named = jnp.sum(
        (groups[None] == jnp.arange(NZ * NY, dtype=I32)[:, None, None]).astype(F32), axis=1
    ).astype(BF16)
    token = jnp.arange(2 * tokens, dtype=I32)
    z, y, part = token // (2 * cut * NY), token // (2 * cut) % NY, token // cut % 2
    block = part * BLOCKS + (y * NZ + z) * BLOCKS // (NY * NZ)
    belongs = (block[:, None] == jnp.arange(2 * BLOCKS, dtype=I32)[None]).astype(BF16)
    fits = jnp.max(jnp.dot(named, belongs, preferred_element_type=F32)) <= SLOTS

    order = [((core + j // NX) % NC) * NX + (xi + j % NX) % NX for j in range(BLOCKS)]
    at = jnp.stack(order).astype(I32)
    bias = (up_bias * (1.0 / BLOCKS)).reshape(clusters // PACK, PACK, neurons)

    def sum_of(part):
        part = part[:NX].astype(F32) + from_peer(part[NX:], "core", 1).astype(F32)
        summed = part[0]
        part = part.astype(BF16)
        for k in range(1, NX):
            summed = summed + from_peer(part[k], "x", -k).astype(F32)
        return jnp.maximum(summed, 0.0).astype(BF16)

    def all_of(own):
        own = jnp.stack([own] + [from_peer(own, "x", k) for k in range(1, NX)])
        return jnp.concatenate([own, from_peer(own, "core", 1)], axis=0)

    own_1 = sum_of(packed_up(at, x_1, up_weight, bias, pos_1))
    part_2 = packed_up(at, x_2, up_weight, bias, pos_2)
    own_1, part_2 = lax.optimization_barrier((own_1, part_2))
    hidden_1 = all_of(own_1)
    hidden_2 = all_of(sum_of(part_2))
    out_1 = packed_down(at, hidden_1, pos_1, down_weight, tokens).reshape(NY, NZ, cut, width)
    out_1 = total(exchange(out_1, "y")).astype(BF16)
    out_2 = packed_down(at, hidden_2, pos_2, down_weight, tokens).reshape(NY, NZ, cut, width)
    out_2 = total(exchange(out_2, "y")).astype(BF16)
    out_1 = ring_total(out_1, "z").astype(BF16)
    out_2 = total(exchange(out_2, "z")).astype(BF16)
    out = jnp.concatenate([out_1, out_2], axis=0)
    whole = (activations, picks, up_weight, up_bias, down_weight)
    return lax.cond(fits, lambda: out, lambda: dense(*whole))


def solution(mesh):
    grid = Mesh(mesh.devices.reshape(NX, NC, NZ, NY), ("x", "core", "z", "y"))
    dp, clus = ("x", "core"), ("z", "y")
    placed = (P(clus, dp), P(), P(clus, dp, None), P(clus, None), P(clus, None, dp))
    return jax.shard_map(
        on_device, mesh=grid, in_specs=placed, out_specs=P(clus, dp), check_vma=False
    )
```

```python
import jax
import jax.numpy as jnp
from jax import lax
from jax.experimental import pallas as pl
from jax.experimental.pallas import tpu as pltpu
from jax.sharding import Mesh
from jax.sharding import PartitionSpec as P

F32, BF16, I32 = jnp.float32, jnp.bfloat16, jnp.int32
NX, NC, NZ, NY = 4, 2, 8, 4
BLOCKS = NX * NC
SLOTS = 192
PACK = 4
TILE = 512
VMEM = 32 << 20


def spread(block, axis):
    peers = lax.axis_size(axis)
    return lax.all_to_all(
        jnp.broadcast_to(block[None], (peers,) + block.shape), axis, split_axis=0, concat_axis=0
    )


def exchange(blocks, axis):
    return lax.all_to_all(blocks, axis, split_axis=0, concat_axis=0)


def total(blocks):
    return jnp.sum(blocks.astype(F32), axis=0)


def from_peer(block, axis, step):
    n = lax.axis_size(axis)
    return lax.ppermute(block, axis, [((i + step) % n, i) for i in range(n)])


def ring_spread(block, axis, beside):
    n = lax.axis_size(axis)
    found = {0: block}
    for k in range(1, n // 2):
        found[k] = from_peer(found[k - 1], axis, 1)
        found[n - k] = from_peer(found[(n + 1 - k) % n], axis, -1)
        if k == 1:
            found[1], found[n - 1], beside = lax.optimization_barrier((found[1], found[n - 1], beside))
    half = block.shape[0] // 2
    low = from_peer(found[n // 2 - 1][:half], axis, 1)
    high = from_peer(found[n // 2 + 1][half:], axis, -1)
    found[n // 2] = jnp.concatenate([low, high])
    return jnp.stack([found[k] for k in range(n)]), beside


def ring_total(blocks, axis, beside):
    n, half = blocks.shape[0], blocks.shape[1] // 2
    low = from_peer(blocks[n // 2][:half], axis, 1).astype(F32)
    high = from_peer(blocks[n // 2][half:], axis, -1).astype(F32)
    down, up = blocks[n // 2 + 1], blocks[n // 2 - 1]
    down = jnp.concatenate([(down[:half] + low).astype(BF16), down[half:]])
    up = jnp.concatenate([up[:half], (up[half:] + high).astype(BF16)])
    for k in range(n // 2 - 2, -1, -1):
        if k == 0:
            down, up, beside = lax.optimization_barrier((down, up, beside))
        down, up = from_peer(down, axis, 1).astype(F32), from_peer(up, axis, -1).astype(F32)
        if k > 0:
            down, up = (blocks[n - k] + down).astype(BF16), (blocks[k] + up).astype(BF16)
    return blocks[0] + down + up, beside


def up_kernel(at_ref, x1_ref, x2_ref, w_ref, bias_ref, pos_ref, out_ref, acc):
    span, neurons = x1_ref.shape[0] // BLOCKS, w_ref.shape[-1]
    slot = lax.broadcasted_iota(I32, (SLOTS, PACK * span), 0)

    @pl.when(pl.program_id(0) == 0)
    def _():
        acc[...] = jnp.zeros_like(acc)

    for part, x_ref in enumerate((x1_ref, x2_ref)):
        pairs = []
        for p in range(0, PACK, 2):
            wide = jnp.concatenate([w_ref[p], w_ref[p + 1]], axis=1)
            bias = jnp.concatenate([bias_ref[0, p : p + 1], bias_ref[0, p + 1 : p + 2]], axis=1)
            pre = jnp.dot(x_ref[...], wide, preferred_element_type=F32)
            pairs.append((pre + bias).astype(BF16))
        for b in range(BLOCKS):
            rows = slice(b * span, (b + 1) * span)
            both = jnp.concatenate(
                [p[rows, k * neurons : (k + 1) * neurons] for p in pairs for k in range(2)], axis=0
            )
            place = pos_ref[0, part * BLOCKS + b : part * BLOCKS + b + 1, :]
            take = jnp.where(slot == place, 1.0, 0.0).astype(BF16)
            acc[b, part * SLOTS : (part + 1) * SLOTS] += jnp.dot(
                take, both, preferred_element_type=F32
            )

    @pl.when(pl.program_id(0) == pl.num_programs(0) - 1)
    def _():
        for j in range(BLOCKS):
            out_ref[j] = acc[at_ref[j]].astype(BF16)


def packed_up(at, x_1, x_2, up_weight, bias, pos):
    clusters, width, neurons = up_weight.shape
    tokens = x_1.shape[0]
    return pl.pallas_call(
        up_kernel,
        grid_spec=pltpu.PrefetchScalarGridSpec(
            num_scalar_prefetch=1,
            grid=(clusters // PACK,),
            in_specs=[
                pl.BlockSpec((tokens, width), lambda i, at: (0, 0)),
                pl.BlockSpec((tokens, width), lambda i, at: (0, 0)),
                pl.BlockSpec((PACK, width, neurons), lambda i, at: (i, 0, 0)),
                pl.BlockSpec((1, PACK, neurons), lambda i, at: (i, 0, 0)),
                pl.BlockSpec((1, 2 * BLOCKS, PACK * tokens // BLOCKS), lambda i, at: (i, 0, 0)),
            ],
            out_specs=pl.BlockSpec((BLOCKS, 2 * SLOTS, neurons), lambda i, at: (0, 0, 0)),
            scratch_shapes=[pltpu.VMEM((BLOCKS, 2 * SLOTS, neurons), F32)],
        ),
        out_shape=jax.ShapeDtypeStruct((BLOCKS, 2 * SLOTS, neurons), BF16),
        compiler_params=pltpu.CompilerParams(vmem_limit_bytes=VMEM),
        cost_estimate=pl.CostEstimate(
            flops=4 * tokens * width * clusters * neurons, bytes_accessed=9 << 20, transcendentals=0
        ),
    )(at, x_1, x_2, up_weight, bias, pos)


def down_kernel(at_ref, packed_ref, pos_ref, w_ref, out_ref, hidden):
    neurons = packed_ref.shape[-1]
    span = hidden.shape[0] // BLOCKS

    @pl.when(pl.program_id(0) == 0)
    def _():
        slot = lax.broadcasted_iota(I32, (SLOTS, PACK * span), 0)
        for j in range(BLOCKS):
            b = at_ref[j]
            to = pl.ds(pl.multiple_of(b * span, span), span)
            for q in range(pos_ref.shape[0]):
                take = jnp.where(slot == pos_ref[q, pl.ds(b, 1), :], 1.0, 0.0).astype(BF16)
                both = lax.dot_general(
                    take, packed_ref[j], (((0,), (0,)), ((), ())), preferred_element_type=F32
                ).astype(BF16)
                for k in range(PACK):
                    c = q * PACK + k
                    hidden[to, c * neurons : (c + 1) * neurons] = both[k * span : (k + 1) * span]

    wide = w_ref[...].reshape(-1, w_ref.shape[-1])
    out_ref[...] = jnp.dot(hidden[...], wide, preferred_element_type=F32).astype(BF16)


def packed_down(at, packed, pos, down_weight, tokens, part):
    clusters, neurons, width = down_weight.shape
    return pl.pallas_call(
        down_kernel,
        grid_spec=pltpu.PrefetchScalarGridSpec(
            num_scalar_prefetch=1,
            grid=(width // TILE,),
            in_specs=[
                pl.BlockSpec((BLOCKS, SLOTS, neurons), lambda n, at: (0, part, 0)),
                pl.BlockSpec((pos.shape[0], BLOCKS, pos.shape[2]), lambda n, at: (0, part, 0)),
                pl.BlockSpec((clusters, neurons, TILE), lambda n, at: (0, 0, n)),
            ],
            out_specs=pl.BlockSpec((tokens, TILE), lambda n, at: (0, n)),
            scratch_shapes=[pltpu.VMEM((tokens, clusters * neurons), BF16)],
        ),
        out_shape=jax.ShapeDtypeStruct((tokens, width), BF16),
        compiler_params=pltpu.CompilerParams(vmem_limit_bytes=VMEM),
        cost_estimate=pl.CostEstimate(
            flops=2 * tokens * clusters * neurons * width, bytes_accessed=7 << 20, transcendentals=0
        ),
    )(at, packed, pos, down_weight)


def slots_of(mask):
    clusters, _, span = mask.shape
    hits = mask.astype(BF16)
    before = jnp.triu(jnp.ones((span, span), BF16), 1)
    ahead = jnp.triu(jnp.ones((clusters, clusters), BF16), 1)
    each = jnp.sum(hits.astype(F32), axis=0).astype(BF16)
    base = jnp.dot(each, before, preferred_element_type=F32)
    within = jnp.einsum("kbt,kc->cbt", hits, ahead, preferred_element_type=F32)
    return jnp.where(mask, base[None] + within, -1.0).astype(I32)


def dense(activations, picks, up_weight, up_bias, down_weight):
    rows, width = activations.shape
    clusters, _, neurons = up_weight.shape
    tokens, span = picks.shape[0], picks.shape[0] // BLOCKS
    x = spread(spread(activations, "y"), "z").reshape(tokens, width)
    part = jnp.einsum("td,cdn->tcn", x, up_weight, preferred_element_type=F32).astype(BF16)
    part = part.reshape(BLOCKS, span, clusters, neurons)
    summed = total(exchange(part, ("x", "core"))) + up_bias[None]
    at = lax.axis_index("x") * NC + lax.axis_index("core")
    group = lax.axis_index("z") * NY + lax.axis_index("y")
    picked = lax.dynamic_slice_in_dim(picks, at * span, span, 0)
    wanted = group * clusters + jnp.arange(clusters, dtype=I32)
    keep = jnp.any(picked[:, :, None] == wanted[None, None, :], axis=1)
    hidden = jnp.where(keep[:, :, None], jnp.maximum(summed, 0.0), 0.0).astype(BF16)
    hidden = spread(hidden, ("x", "core")).reshape(tokens, clusters, neurons)
    out = jnp.einsum("tcn,cnd->td", hidden, down_weight, preferred_element_type=F32)
    out = exchange(out.astype(BF16).reshape(NZ, NY, rows, width), "z")
    out = exchange(total(out).astype(BF16), "y")
    return total(out).astype(BF16)


def on_device(activations, picks, up_weight, up_bias, down_weight):
    rows, width = activations.shape
    clusters, _, neurons = up_weight.shape
    cut = rows // 2
    tokens = NZ * NY * cut
    span = tokens // BLOCKS
    core, xi = lax.axis_index("core"), lax.axis_index("x")
    zi, yi = lax.axis_index("z"), lax.axis_index("y")

    first = spread(activations[:cut], "z")
    near = jnp.stack([activations[cut:]] + [from_peer(activations[cut:], "y", k) for k in range(1, NY)])
    x_2, first = ring_spread(near, "z", first)
    x_1, x_2 = spread(first, "y").reshape(tokens, width), x_2.reshape(tokens, width)

    wanted = (zi * NY + yi) * clusters + jnp.arange(clusters, dtype=I32)
    mask = jnp.any(picks.T[None, :, :] == wanted[:, None, None], axis=1)
    mask = mask.reshape(clusters, NZ, NY, 2, cut)
    mask_1 = mask[:, :, :, 0].transpose(0, 2, 1, 3).reshape(clusters, BLOCKS, span)
    mask_2 = jnp.roll(mask[:, :, :, 1], (-zi, -yi), axis=(1, 2)).reshape(clusters, BLOCKS, span)
    pos = slots_of(jnp.concatenate([mask_1, mask_2], axis=1))
    pos = pos.reshape(clusters // PACK, PACK, 2 * BLOCKS, span).transpose(0, 2, 1, 3)
    pos = pos.reshape(clusters // PACK, 2 * BLOCKS, PACK * span)

    groups = picks.T // clusters
    named = jnp.sum(
        (groups[None] == jnp.arange(NZ * NY, dtype=I32)[:, None, None]).astype(F32), axis=1
    ).astype(BF16)
    token = jnp.arange(2 * tokens, dtype=I32)
    z, y, part = token // (2 * cut * NY), token // (2 * cut) % NY, token // cut % 2
    block = jnp.where(part == 0, (y * NZ + z) * BLOCKS // (NY * NZ), BLOCKS + z * BLOCKS // NZ)
    belongs = (block[:, None] == jnp.arange(2 * BLOCKS, dtype=I32)[None]).astype(BF16)
    fits = jnp.max(jnp.dot(named, belongs, preferred_element_type=F32)) <= SLOTS

    order = [((core + j // NX) % NC) * NX + (xi + j % NX) % NX for j in range(BLOCKS)]
    at = jnp.stack(order).astype(I32)
    bias = (up_bias * (1.0 / BLOCKS)).reshape(clusters // PACK, PACK, neurons)

    def sum_of(part):
        part = part[:NX].astype(F32) + from_peer(part[NX:], "core", 1).astype(F32)
        summed = part[0]
        part = part.astype(BF16)
        for k in range(1, NX):
            summed = summed + from_peer(part[k], "x", -k).astype(F32)
        return jnp.maximum(summed, 0.0).astype(BF16)

    def all_of(own):
        own = jnp.stack([own] + [from_peer(own, "x", k) for k in range(1, NX)])
        return jnp.concatenate([own, from_peer(own, "core", 1)], axis=0)

    packed = all_of(sum_of(packed_up(at, x_1, x_2, up_weight, bias, pos)))
    out_1 = packed_down(at, packed, pos, down_weight, tokens, 0).reshape(NY, NZ, cut, width)
    out_2 = packed_down(at, packed, pos, down_weight, tokens, 1).reshape(NZ, NY, cut, width)
    out_1 = total(exchange(out_1, "y")).astype(BF16)
    out_2, out_1 = ring_total(out_2, "z", out_1)
    out_1 = total(exchange(out_1, "z")).astype(BF16)
    out_2 = out_2.astype(BF16)
    done = out_2[0].astype(F32)
    for k in range(1, NY):
        done = done + from_peer(out_2[k], "y", -k).astype(F32)
    out = jnp.concatenate([out_1, done.astype(BF16)], axis=0)
    whole = (activations, picks, up_weight, up_bias, down_weight)
    return lax.cond(fits, lambda: out, lambda: dense(*whole))


def solution(mesh):
    grid = Mesh(mesh.devices.reshape(NX, NC, NZ, NY), ("x", "core", "z", "y"))
    dp, clus = ("x", "core"), ("z", "y")
    placed = (P(clus, dp), P(), P(clus, dp, None), P(clus, None), P(clus, None, dp))
    return jax.shard_map(
        on_device, mesh=grid, in_specs=placed, out_specs=P(clus, dp), check_vma=False
    )
```

```python
import jax
import jax.numpy as jnp
from jax import lax
from jax.experimental import pallas as pl
from jax.experimental.pallas import tpu as pltpu
from jax.sharding import Mesh
from jax.sharding import PartitionSpec as P

F32, BF16, I32 = jnp.float32, jnp.bfloat16, jnp.int32
NX, NC, NZ, NY = 4, 2, 8, 4
BLOCKS = NX * NC
SLOTS = 192
PACK = 4
TILE = 512
VMEM = 32 << 20


def spread(block, axis):
    peers = lax.axis_size(axis)
    return lax.all_to_all(
        jnp.broadcast_to(block[None], (peers,) + block.shape), axis, split_axis=0, concat_axis=0
    )


def exchange(blocks, axis):
    return lax.all_to_all(blocks, axis, split_axis=0, concat_axis=0)


def total(blocks):
    return jnp.sum(blocks.astype(F32), axis=0)


def from_peer(block, axis, step):
    n = lax.axis_size(axis)
    return lax.ppermute(block, axis, [((i + step) % n, i) for i in range(n)])


def ring_spread(block, axis, beside):
    n = lax.axis_size(axis)
    found = {0: block}
    for k in range(1, n // 2):
        found[k] = from_peer(found[k - 1], axis, 1)
        found[n - k] = from_peer(found[(n + 1 - k) % n], axis, -1)
    half = block.shape[0] // 2
    low, high = found[n // 2 - 1], found[n // 2 + 1]
    low, high, beside = lax.optimization_barrier((low, high, beside))
    low, high = from_peer(low[:half], axis, 1), from_peer(high[half:], axis, -1)
    found[n // 2] = jnp.concatenate([low, high])
    return jnp.stack([found[k] for k in range(n)]), beside


def ring_total(blocks, axis, beside):
    n, half = blocks.shape[0], blocks.shape[1] // 2
    low = from_peer(blocks[n // 2][:half], axis, 1).astype(F32)
    high = from_peer(blocks[n // 2][half:], axis, -1).astype(F32)
    down, up = blocks[n // 2 + 1], blocks[n // 2 - 1]
    down = jnp.concatenate([(down[:half] + low).astype(BF16), down[half:]])
    up = jnp.concatenate([up[:half], (up[half:] + high).astype(BF16)])
    for k in range(n // 2 - 2, -1, -1):
        if k == 0:
            down, up, beside = lax.optimization_barrier((down, up, beside))
        down, up = from_peer(down, axis, 1).astype(F32), from_peer(up, axis, -1).astype(F32)
        if k > 0:
            down, up = (blocks[n - k] + down).astype(BF16), (blocks[k] + up).astype(BF16)
    return blocks[0] + down + up, beside


def up_kernel(at_ref, x_ref, w_ref, bias_ref, pos_ref, out_ref, acc):
    span, neurons = x_ref.shape[0] // BLOCKS, w_ref.shape[-1]
    slot = lax.broadcasted_iota(I32, (SLOTS, PACK * span), 0)

    @pl.when(pl.program_id(0) == 0)
    def _():
        acc[...] = jnp.zeros_like(acc)

    pairs = []
    for p in range(0, PACK, 2):
        wide = jnp.concatenate([w_ref[p], w_ref[p + 1]], axis=1)
        bias = jnp.concatenate([bias_ref[0, p : p + 1], bias_ref[0, p + 1 : p + 2]], axis=1)
        pre = jnp.dot(x_ref[...], wide, preferred_element_type=F32)
        pairs.append((pre + bias).astype(BF16))
    for b in range(BLOCKS):
        rows = slice(b * span, (b + 1) * span)
        both = jnp.concatenate(
            [p[rows, k * neurons : (k + 1) * neurons] for p in pairs for k in range(2)], axis=0
        )
        take = jnp.where(slot == pos_ref[0, b : b + 1, :], 1.0, 0.0).astype(BF16)
        acc[b] += jnp.dot(take, both, preferred_element_type=F32)

    @pl.when(pl.program_id(0) == pl.num_programs(0) - 1)
    def _():
        for j in range(BLOCKS):
            out_ref[j] = acc[at_ref[j]].astype(BF16)


def packed_up(at, x, up_weight, bias, pos, part):
    clusters, width, neurons = up_weight.shape
    tokens = x.shape[0]
    return pl.pallas_call(
        up_kernel,
        grid_spec=pltpu.PrefetchScalarGridSpec(
            num_scalar_prefetch=1,
            grid=(clusters // PACK,),
            in_specs=[
                pl.BlockSpec((tokens, width), lambda i, at: (0, 0)),
                pl.BlockSpec((PACK, width, neurons), lambda i, at: (i, 0, 0)),
                pl.BlockSpec((1, PACK, neurons), lambda i, at: (i, 0, 0)),
                pl.BlockSpec((1, BLOCKS, PACK * tokens // BLOCKS), lambda i, at: (i, part, 0)),
            ],
            out_specs=pl.BlockSpec((BLOCKS, SLOTS, neurons), lambda i, at: (0, 0, 0)),
            scratch_shapes=[pltpu.VMEM((BLOCKS, SLOTS, neurons), F32)],
        ),
        out_shape=jax.ShapeDtypeStruct((BLOCKS, SLOTS, neurons), BF16),
        compiler_params=pltpu.CompilerParams(vmem_limit_bytes=VMEM),
        cost_estimate=pl.CostEstimate(
            flops=4 * tokens * width * clusters * neurons, bytes_accessed=9 << 20, transcendentals=0
        ),
    )(at, x, up_weight, bias, pos)


def down_kernel(at_ref, packed_ref, pos_ref, w_ref, out_ref, hidden):
    neurons = packed_ref.shape[-1]
    span = hidden.shape[0] // BLOCKS

    @pl.when(pl.program_id(0) == 0)
    def _():
        slot = lax.broadcasted_iota(I32, (SLOTS, PACK * span), 0)
        for j in range(BLOCKS):
            b = at_ref[j]
            to = pl.ds(pl.multiple_of(b * span, span), span)
            for q in range(pos_ref.shape[0]):
                take = jnp.where(slot == pos_ref[q, pl.ds(b, 1), :], 1.0, 0.0).astype(BF16)
                both = lax.dot_general(
                    take, packed_ref[j], (((0,), (0,)), ((), ())), preferred_element_type=F32
                ).astype(BF16)
                for k in range(PACK):
                    c = q * PACK + k
                    hidden[to, c * neurons : (c + 1) * neurons] = both[k * span : (k + 1) * span]

    wide = w_ref[...].reshape(-1, w_ref.shape[-1])
    out_ref[...] = jnp.dot(hidden[...], wide, preferred_element_type=F32).astype(BF16)


def packed_down(at, packed, pos, down_weight, tokens, part):
    clusters, neurons, width = down_weight.shape
    return pl.pallas_call(
        down_kernel,
        grid_spec=pltpu.PrefetchScalarGridSpec(
            num_scalar_prefetch=1,
            grid=(width // TILE,),
            in_specs=[
                pl.BlockSpec((BLOCKS, SLOTS, neurons), lambda n, at: (0, part, 0)),
                pl.BlockSpec((pos.shape[0], BLOCKS, pos.shape[2]), lambda n, at: (0, part, 0)),
                pl.BlockSpec((clusters, neurons, TILE), lambda n, at: (0, 0, n)),
            ],
            out_specs=pl.BlockSpec((tokens, TILE), lambda n, at: (0, n)),
            scratch_shapes=[pltpu.VMEM((tokens, clusters * neurons), BF16)],
        ),
        out_shape=jax.ShapeDtypeStruct((tokens, width), BF16),
        compiler_params=pltpu.CompilerParams(vmem_limit_bytes=VMEM),
        cost_estimate=pl.CostEstimate(
            flops=2 * tokens * clusters * neurons * width, bytes_accessed=7 << 20, transcendentals=0
        ),
    )(at, packed, pos, down_weight)


def slots_of(mask):
    clusters, _, span = mask.shape
    hits = mask.astype(BF16)
    before = jnp.triu(jnp.ones((span, span), BF16), 1)
    ahead = jnp.triu(jnp.ones((clusters, clusters), BF16), 1)
    each = jnp.sum(hits.astype(F32), axis=0).astype(BF16)
    base = jnp.dot(each, before, preferred_element_type=F32)
    within = jnp.einsum("kbt,kc->cbt", hits, ahead, preferred_element_type=F32)
    return jnp.where(mask, base[None] + within, -1.0).astype(I32)


def dense(activations, picks, up_weight, up_bias, down_weight):
    rows, width = activations.shape
    clusters, _, neurons = up_weight.shape
    tokens, span = picks.shape[0], picks.shape[0] // BLOCKS
    x = spread(spread(activations, "y"), "z").reshape(tokens, width)
    part = jnp.einsum("td,cdn->tcn", x, up_weight, preferred_element_type=F32).astype(BF16)
    part = part.reshape(BLOCKS, span, clusters, neurons)
    summed = total(exchange(part, ("x", "core"))) + up_bias[None]
    at = lax.axis_index("x") * NC + lax.axis_index("core")
    group = lax.axis_index("z") * NY + lax.axis_index("y")
    picked = lax.dynamic_slice_in_dim(picks, at * span, span, 0)
    wanted = group * clusters + jnp.arange(clusters, dtype=I32)
    keep = jnp.any(picked[:, :, None] == wanted[None, None, :], axis=1)
    hidden = jnp.where(keep[:, :, None], jnp.maximum(summed, 0.0), 0.0).astype(BF16)
    hidden = spread(hidden, ("x", "core")).reshape(tokens, clusters, neurons)
    out = jnp.einsum("tcn,cnd->td", hidden, down_weight, preferred_element_type=F32)
    out = exchange(out.astype(BF16).reshape(NZ, NY, rows, width), "z")
    out = exchange(total(out).astype(BF16), "y")
    return total(out).astype(BF16)


def on_device(activations, picks, up_weight, up_bias, down_weight):
    rows, width = activations.shape
    clusters, _, neurons = up_weight.shape
    cut = rows // 2
    tokens = NZ * NY * cut
    span = tokens // BLOCKS
    core, xi = lax.axis_index("core"), lax.axis_index("x")
    zi, yi = lax.axis_index("z"), lax.axis_index("y")

    first, second = activations[:cut], activations[cut:]
    first = spread(first, "z")

    wanted = (zi * NY + yi) * clusters + jnp.arange(clusters, dtype=I32)
    mask = jnp.any(picks.T[None, :, :] == wanted[:, None, None], axis=1)
    mask = mask.reshape(clusters, NZ, NY, 2, cut)
    mask_1 = mask[:, :, :, 0].transpose(0, 2, 1, 3).reshape(clusters, BLOCKS, span)
    mask_2 = jnp.roll(mask[:, :, :, 1], (-zi, -yi), axis=(1, 2)).reshape(clusters, BLOCKS, span)
    pos = slots_of(jnp.concatenate([mask_1, mask_2], axis=1))
    pos = pos.reshape(clusters // PACK, PACK, 2 * BLOCKS, span).transpose(0, 2, 1, 3)
    pos = pos.reshape(clusters // PACK, 2 * BLOCKS, PACK * span)

    second, pos = lax.optimization_barrier((second, pos))
    near = jnp.stack([second] + [from_peer(second, "y", k) for k in range(1, NY)])
    near, first = lax.optimization_barrier((near, first))
    x_1 = spread(first, "y").reshape(tokens, width)
    x_2, x_1 = ring_spread(near, "z", x_1)
    x_2 = x_2.reshape(tokens, width)

    groups = picks.T // clusters
    named = jnp.sum(
        (groups[None] == jnp.arange(NZ * NY, dtype=I32)[:, None, None]).astype(F32), axis=1
    ).astype(BF16)
    token = jnp.arange(2 * tokens, dtype=I32)
    z, y, part = token // (2 * cut * NY), token // (2 * cut) % NY, token // cut % 2
    block = jnp.where(part == 0, (y * NZ + z) * BLOCKS // (NY * NZ), BLOCKS + z * BLOCKS // NZ)
    belongs = (block[:, None] == jnp.arange(2 * BLOCKS, dtype=I32)[None]).astype(BF16)
    fits = jnp.max(jnp.dot(named, belongs, preferred_element_type=F32)) <= SLOTS

    order = [((core + j // NX) % NC) * NX + (xi + j % NX) % NX for j in range(BLOCKS)]
    at = jnp.stack(order).astype(I32)
    bias = (up_bias * (1.0 / BLOCKS)).reshape(clusters // PACK, PACK, neurons)

    def pair_of(x, part):
        rows = packed_up(at, x, up_weight, bias, pos, part)
        return rows[:NX].astype(F32) + from_peer(rows[NX:], "core", 1).astype(F32)

    def sum_of(rows):
        summed = rows[0]
        rows = rows.astype(BF16)
        for k in range(1, NX):
            summed = summed + from_peer(rows[k], "x", -k).astype(F32)
        return jnp.maximum(summed, 0.0).astype(BF16)

    def all_of(own):
        own = jnp.stack([own] + [from_peer(own, "x", k) for k in range(1, NX)])
        return jnp.concatenate([own, from_peer(own, "core", 1)], axis=0)

    rows_1, rows_2 = pair_of(x_1, 0), pair_of(x_2, 1)
    packed = all_of(sum_of(jnp.concatenate([rows_1, rows_2], axis=1)))
    out_1 = packed_down(at, packed, pos, down_weight, tokens, 0).reshape(NY, NZ, cut, width)
    out_2 = packed_down(at, packed, pos, down_weight, tokens, 1).reshape(NZ, NY, cut, width)
    out_1 = total(exchange(out_1, "y")).astype(BF16)
    out_2, out_1 = ring_total(out_2, "z", out_1)
    out_1 = total(exchange(out_1, "z")).astype(BF16)
    out_2 = out_2.astype(BF16)
    done = out_2[0].astype(F32)
    for k in range(1, NY):
        done = done + from_peer(out_2[k], "y", -k).astype(F32)
    out = jnp.concatenate([out_1, done.astype(BF16)], axis=0)
    whole = (activations, picks, up_weight, up_bias, down_weight)
    return lax.cond(fits, lambda: out, lambda: dense(*whole))


def solution(mesh):
    grid = Mesh(mesh.devices.reshape(NX, NC, NZ, NY), ("x", "core", "z", "y"))
    dp, clus = ("x", "core"), ("z", "y")
    placed = (P(clus, dp), P(), P(clus, dp, None), P(clus, None), P(clus, None, dp))
    return jax.shard_map(
        on_device, mesh=grid, in_specs=placed, out_specs=P(clus, dp), check_vma=False
    )
```

```python
import jax
import jax.numpy as jnp
from jax import lax
from jax.experimental import pallas as pl
from jax.experimental.pallas import tpu as pltpu
from jax.sharding import Mesh
from jax.sharding import PartitionSpec as P

F32, BF16, I32 = jnp.float32, jnp.bfloat16, jnp.int32
NX, NC, NZ, NY = 4, 2, 8, 4
BLOCKS = NX * NC
SLOTS = 192
PACK = 4
TILE = 512
VMEM = 32 << 20


def spread(block, axis):
    peers = lax.axis_size(axis)
    return lax.all_to_all(
        jnp.broadcast_to(block[None], (peers,) + block.shape), axis, split_axis=0, concat_axis=0
    )


def exchange(blocks, axis):
    return lax.all_to_all(blocks, axis, split_axis=0, concat_axis=0)


def total(blocks):
    return jnp.sum(blocks.astype(F32), axis=0)


def from_peer(block, axis, step):
    n = lax.axis_size(axis)
    return lax.ppermute(block, axis, [((i + step) % n, i) for i in range(n)])


def ring_spread(block, axis, beside):
    n = lax.axis_size(axis)
    found = {0: block}
    for k in range(1, n // 2):
        found[k] = from_peer(found[k - 1], axis, 1)
        found[n - k] = from_peer(found[(n + 1 - k) % n], axis, -1)
    half = block.shape[0] // 2
    low, high = found[n // 2 - 1], found[n // 2 + 1]
    low, high, beside = lax.optimization_barrier((low, high, beside))
    low, high = from_peer(low[:half], axis, 1), from_peer(high[half:], axis, -1)
    found[n // 2] = jnp.concatenate([low, high])
    return jnp.stack([found[k] for k in range(n)]), beside


def ring_total(blocks, axis, beside):
    n, half = blocks.shape[0], blocks.shape[1] // 2
    low = from_peer(blocks[n // 2][:half], axis, 1).astype(F32)
    high = from_peer(blocks[n // 2][half:], axis, -1).astype(F32)
    down, up = blocks[n // 2 + 1], blocks[n // 2 - 1]
    down = jnp.concatenate([(down[:half] + low).astype(BF16), down[half:]])
    up = jnp.concatenate([up[:half], (up[half:] + high).astype(BF16)])
    for k in range(n // 2 - 2, -1, -1):
        if k == 0:
            down, up, beside = lax.optimization_barrier((down, up, beside))
        down, up = from_peer(down, axis, 1).astype(F32), from_peer(up, axis, -1).astype(F32)
        if k > 0:
            down, up = (blocks[n - k] + down).astype(BF16), (blocks[k] + up).astype(BF16)
    return blocks[0] + down + up, beside


def up_kernel(at_ref, x_ref, w_ref, bias_ref, pos_ref, out_ref, acc):
    span, neurons = x_ref.shape[0] // BLOCKS, w_ref.shape[-1]
    slot = lax.broadcasted_iota(I32, (SLOTS, PACK * span), 0)

    @pl.when(pl.program_id(0) == 0)
    def _():
        acc[...] = jnp.zeros_like(acc)

    pairs = []
    for p in range(0, PACK, 2):
        wide = jnp.concatenate([w_ref[p], w_ref[p + 1]], axis=1)
        bias = jnp.concatenate([bias_ref[0, p : p + 1], bias_ref[0, p + 1 : p + 2]], axis=1)
        pre = jnp.dot(x_ref[...], wide, preferred_element_type=F32)
        pairs.append((pre + bias).astype(BF16))
    for b in range(BLOCKS):
        rows = slice(b * span, (b + 1) * span)
        both = jnp.concatenate(
            [p[rows, k * neurons : (k + 1) * neurons] for p in pairs for k in range(2)], axis=0
        )
        take = jnp.where(slot == pos_ref[0, b : b + 1, :], 1.0, 0.0).astype(BF16)
        acc[b] += jnp.dot(take, both, preferred_element_type=F32)

    @pl.when(pl.program_id(0) == pl.num_programs(0) - 1)
    def _():
        for j in range(BLOCKS):
            out_ref[j] = acc[at_ref[j]].astype(BF16)


def packed_up(at, x, up_weight, bias, pos, part):
    clusters, width, neurons = up_weight.shape
    tokens = x.shape[0]
    return pl.pallas_call(
        up_kernel,
        grid_spec=pltpu.PrefetchScalarGridSpec(
            num_scalar_prefetch=1,
            grid=(clusters // PACK,),
            in_specs=[
                pl.BlockSpec((tokens, width), lambda i, at: (0, 0)),
                pl.BlockSpec((PACK, width, neurons), lambda i, at: (i, 0, 0)),
                pl.BlockSpec((1, PACK, neurons), lambda i, at: (i, 0, 0)),
                pl.BlockSpec((1, BLOCKS, PACK * tokens // BLOCKS), lambda i, at: (i, part, 0)),
            ],
            out_specs=pl.BlockSpec((BLOCKS, SLOTS, neurons), lambda i, at: (0, 0, 0)),
            scratch_shapes=[pltpu.VMEM((BLOCKS, SLOTS, neurons), F32)],
        ),
        out_shape=jax.ShapeDtypeStruct((BLOCKS, SLOTS, neurons), BF16),
        compiler_params=pltpu.CompilerParams(vmem_limit_bytes=VMEM),
        cost_estimate=pl.CostEstimate(
            flops=4 * tokens * width * clusters * neurons, bytes_accessed=9 << 20, transcendentals=0
        ),
    )(at, x, up_weight, bias, pos)


def down_kernel(at_ref, packed_ref, pos_ref, w_ref, out_ref, hidden):
    neurons = packed_ref.shape[-1]
    span = hidden.shape[0] // BLOCKS

    @pl.when(pl.program_id(0) == 0)
    def _():
        slot = lax.broadcasted_iota(I32, (SLOTS, PACK * span), 0)
        @pl.loop(0, BLOCKS)
        def _(j):
            b = at_ref[j]
            to = pl.ds(pl.multiple_of(b * span, span), span)
            for q in range(pos_ref.shape[0]):
                take = jnp.where(slot == pos_ref[q, pl.ds(b, 1), :], 1.0, 0.0).astype(BF16)
                both = lax.dot_general(
                    take, packed_ref[j], (((0,), (0,)), ((), ())), preferred_element_type=F32
                ).astype(BF16)
                for k in range(PACK):
                    c = q * PACK + k
                    hidden[to, c * neurons : (c + 1) * neurons] = both[k * span : (k + 1) * span]

    wide = w_ref[...].reshape(-1, w_ref.shape[-1])
    out_ref[...] = jnp.dot(hidden[...], wide, preferred_element_type=F32).astype(BF16)


def packed_down(at, packed, pos, down_weight, tokens, part):
    clusters, neurons, width = down_weight.shape
    return pl.pallas_call(
        down_kernel,
        grid_spec=pltpu.PrefetchScalarGridSpec(
            num_scalar_prefetch=1,
            grid=(width // TILE,),
            in_specs=[
                pl.BlockSpec((BLOCKS, SLOTS, neurons), lambda n, at: (0, part, 0)),
                pl.BlockSpec((pos.shape[0], BLOCKS, pos.shape[2]), lambda n, at: (0, part, 0)),
                pl.BlockSpec((clusters, neurons, TILE), lambda n, at: (0, 0, n)),
            ],
            out_specs=pl.BlockSpec((tokens, TILE), lambda n, at: (0, n)),
            scratch_shapes=[pltpu.VMEM((tokens, clusters * neurons), BF16)],
        ),
        out_shape=jax.ShapeDtypeStruct((tokens, width), BF16),
        compiler_params=pltpu.CompilerParams(vmem_limit_bytes=VMEM),
        cost_estimate=pl.CostEstimate(
            flops=2 * tokens * clusters * neurons * width, bytes_accessed=7 << 20, transcendentals=0
        ),
    )(at, packed, pos, down_weight)


def slots_of(mask):
    clusters, _, span = mask.shape
    hits = mask.astype(BF16)
    before = jnp.triu(jnp.ones((span, span), BF16), 1)
    ahead = jnp.triu(jnp.ones((clusters, clusters), BF16), 1)
    each = jnp.sum(hits.astype(F32), axis=0).astype(BF16)
    base = jnp.dot(each, before, preferred_element_type=F32)
    within = jnp.einsum("kbt,kc->cbt", hits, ahead, preferred_element_type=F32)
    return jnp.where(mask, base[None] + within, -1.0).astype(I32)


def loop_spread(block, axes):
    n, me = lax.axis_size(axes), lax.axis_index(axes)

    def step(k, held):
        block, found = held
        block = from_peer(block, axes, 1)
        return block, lax.dynamic_update_index_in_dim(found, block, (me + k) % n, 0)

    found = lax.dynamic_update_index_in_dim(jnp.zeros((n,) + block.shape, block.dtype), block, me, 0)
    return lax.fori_loop(1, n, step, (block, found))[1]


def loop_total(blocks, axes):
    n, me = lax.axis_size(axes), lax.axis_index(axes)

    def step(k, sum):
        sum = from_peer(sum, axes, 1)
        return sum + lax.dynamic_index_in_dim(blocks, (me + k) % n, 0, False).astype(F32)

    first = lax.dynamic_index_in_dim(blocks, (me + 1) % n, 0, False).astype(F32)
    return lax.fori_loop(2, n + 1, step, first)


def dense(activations, picks, up_weight, up_bias, down_weight):
    rows, width = activations.shape
    clusters, _, neurons = up_weight.shape
    tokens, span = picks.shape[0], picks.shape[0] // BLOCKS
    dp, clus = ("x", "core"), ("z", "y")
    x = loop_spread(activations, clus).reshape(tokens, width)
    picked = lax.dynamic_slice_in_dim(picks, lax.axis_index(dp) * span, span, 0)

    def cluster(c, out):
        part = jnp.dot(x, up_weight[c], preferred_element_type=F32)
        summed = loop_total(part.reshape(BLOCKS, span, neurons), dp) + up_bias[c]
        keep = jnp.any(picked == lax.axis_index(clus) * clusters + c, axis=1, keepdims=True)
        hidden = jnp.where(keep, jnp.maximum(summed, 0.0), 0.0).astype(BF16)
        hidden = loop_spread(hidden, dp).reshape(tokens, neurons)
        return out + jnp.dot(hidden, down_weight[c], preferred_element_type=F32)

    out = lax.fori_loop(0, clusters, cluster, jnp.zeros((tokens, width), F32)).astype(BF16)
    return loop_total(out.reshape(-1, rows, width), clus).astype(BF16)


def on_device(activations, picks, up_weight, up_bias, down_weight):
    rows, width = activations.shape
    clusters, _, neurons = up_weight.shape
    cut = rows // 2
    tokens = NZ * NY * cut
    span = tokens // BLOCKS
    core, xi = lax.axis_index("core"), lax.axis_index("x")
    zi, yi = lax.axis_index("z"), lax.axis_index("y")

    first, second = activations[:cut], activations[cut:]
    first = spread(first, "z")

    wanted = (zi * NY + yi) * clusters + jnp.arange(clusters, dtype=I32)
    mask = jnp.any(picks.T[None, :, :] == wanted[:, None, None], axis=1)
    mask = mask.reshape(clusters, NZ, NY, 2, cut)
    mask_1 = mask[:, :, :, 0].transpose(0, 2, 1, 3).reshape(clusters, BLOCKS, span)
    mask_2 = jnp.roll(mask[:, :, :, 1], (-zi, -yi), axis=(1, 2)).reshape(clusters, BLOCKS, span)
    pos = slots_of(jnp.concatenate([mask_1, mask_2], axis=1))
    pos = pos.reshape(clusters // PACK, PACK, 2 * BLOCKS, span).transpose(0, 2, 1, 3)
    pos = pos.reshape(clusters // PACK, 2 * BLOCKS, PACK * span)

    groups = picks.T // clusters
    named = jnp.sum(
        (groups[None] == jnp.arange(NZ * NY, dtype=I32)[:, None, None]).astype(F32), axis=1
    ).astype(BF16)
    token = jnp.arange(2 * tokens, dtype=I32)
    z, y, part = token // (2 * cut * NY), token // (2 * cut) % NY, token // cut % 2
    block = jnp.where(part == 0, (y * NZ + z) * BLOCKS // (NY * NZ), BLOCKS + z * BLOCKS // NZ)
    belongs = (block[:, None] == jnp.arange(2 * BLOCKS, dtype=I32)[None]).astype(BF16)
    room = jnp.max(jnp.dot(named, belongs, preferred_element_type=F32))

    near = jnp.stack([second] + [from_peer(second, "y", k) for k in range(1, NY)])
    near, first = lax.optimization_barrier((near, first))
    x_1 = spread(first, "y").reshape(tokens, width)
    x_2, (x_1, room) = ring_spread(near, "z", (x_1, room))
    x_2 = x_2.reshape(tokens, width)

    order = [((core + j // NX) % NC) * NX + (xi + j % NX) % NX for j in range(BLOCKS)]
    at = jnp.stack(order).astype(I32)
    bias = (up_bias * (1.0 / BLOCKS)).reshape(clusters // PACK, PACK, neurons)

    def pair_of(x, part):
        rows = packed_up(at, x, up_weight, bias, pos, part)
        return rows[:NX].astype(F32) + from_peer(rows[NX:], "core", 1).astype(F32)

    def sum_of(rows):
        summed = rows[0]
        rows = rows.astype(BF16)
        for k in range(1, NX):
            summed = summed + from_peer(rows[k], "x", -k).astype(F32)
        return jnp.maximum(summed, 0.0).astype(BF16)

    def all_of(own):
        own = jnp.stack([own] + [from_peer(own, "x", k) for k in range(1, NX)])
        return jnp.concatenate([own, from_peer(own, "core", 1)], axis=0)

    rows_1, rows_2 = pair_of(x_1, 0), pair_of(x_2, 1)
    packed = all_of(sum_of(jnp.concatenate([rows_1, rows_2], axis=1)))
    out_1 = packed_down(at, packed, pos, down_weight, tokens, 0).reshape(NY, NZ, cut, width)
    out_2 = packed_down(at, packed, pos, down_weight, tokens, 1).reshape(NZ, NY, cut, width)
    out_1 = total(exchange(out_1, "y")).astype(BF16)
    out_2, out_1 = ring_total(out_2, "z", out_1)
    out_1 = total(exchange(out_1, "z")).astype(BF16)
    out_2 = out_2.astype(BF16)
    done = out_2[0].astype(F32)
    for k in range(1, NY):
        done = done + from_peer(out_2[k], "y", -k).astype(F32)
    out = jnp.concatenate([out_1, done.astype(BF16)], axis=0)
    whole = (activations, picks, up_weight, up_bias, down_weight)
    return lax.cond(room <= SLOTS, lambda: out, lambda: dense(*whole))


def solution(mesh):
    grid = Mesh(mesh.devices.reshape(NX, NC, NZ, NY), ("x", "core", "z", "y"))
    dp, clus = ("x", "core"), ("z", "y")
    placed = (P(clus, dp), P(), P(clus, dp, None), P(clus, None), P(clus, None, dp))
    return jax.shard_map(
        on_device, mesh=grid, in_specs=placed, out_specs=P(clus, dp), check_vma=False
    )
```

```python
import jax
import jax.numpy as jnp
from jax import lax
from jax.experimental import pallas as pl
from jax.experimental.pallas import tpu as pltpu
from jax.sharding import Mesh
from jax.sharding import PartitionSpec as P

F32, BF16, I32 = jnp.float32, jnp.bfloat16, jnp.int32
NX, NC, NZ, NY = 4, 2, 8, 4
BLOCKS = NX * NC
SLOTS = 192
PACK = 4
TILE = 512
VMEM = 32 << 20


def spread(block, axis):
    peers = lax.axis_size(axis)
    return lax.all_to_all(
        jnp.broadcast_to(block[None], (peers,) + block.shape), axis, split_axis=0, concat_axis=0
    )


def exchange(blocks, axis):
    return lax.all_to_all(blocks, axis, split_axis=0, concat_axis=0)


def total(blocks):
    return jnp.sum(blocks.astype(F32), axis=0)


def from_peer(block, axis, step):
    n = lax.axis_size(axis)
    return lax.ppermute(block, axis, [((i + step) % n, i) for i in range(n)])


def ring_spread(block, axis, beside):
    n = lax.axis_size(axis)
    found = {0: block}
    for k in range(1, n // 2):
        found[k] = from_peer(found[k - 1], axis, 1)
        found[n - k] = from_peer(found[(n + 1 - k) % n], axis, -1)
    last, beside = lax.optimization_barrier((found[n // 2 - 1], beside))
    found[n // 2] = from_peer(last, axis, 1)
    return jnp.stack([found[k] for k in range(n)]), beside


def ring_total(blocks, axis, beside):
    n = blocks.shape[0]
    down, up = blocks[n // 2], blocks[n // 2 - 1]
    for k in range(n // 2 - 1, 0, -1):
        down = (blocks[n - k] + from_peer(down, axis, 1).astype(F32)).astype(BF16)
        if k < n // 2 - 1:
            up = (blocks[k] + from_peer(up, axis, -1).astype(F32)).astype(BF16)
    down, up, beside = lax.optimization_barrier((down, up, beside))
    mine = blocks[0] + from_peer(down, axis, 1).astype(F32) + from_peer(up, axis, -1).astype(F32)
    return mine, beside


def up_kernel(at_ref, x_ref, w_ref, bias_ref, pos_ref, out_ref, acc):
    span, neurons = x_ref.shape[0] // BLOCKS, w_ref.shape[-1]
    slot = lax.broadcasted_iota(I32, (SLOTS, PACK * span), 0)

    @pl.when(pl.program_id(0) == 0)
    def _():
        acc[...] = jnp.zeros_like(acc)

    pairs = []
    for p in range(0, PACK, 2):
        wide = jnp.concatenate([w_ref[p], w_ref[p + 1]], axis=1)
        bias = jnp.concatenate([bias_ref[0, p : p + 1], bias_ref[0, p + 1 : p + 2]], axis=1)
        pre = jnp.dot(x_ref[...], wide, preferred_element_type=F32)
        pairs.append((pre + bias).astype(BF16))
    for b in range(BLOCKS):
        rows = slice(b * span, (b + 1) * span)
        both = jnp.concatenate(
            [p[rows, k * neurons : (k + 1) * neurons] for p in pairs for k in range(2)], axis=0
        )
        take = jnp.where(slot == pos_ref[0, b : b + 1, :], 1.0, 0.0).astype(BF16)
        acc[b] += jnp.dot(take, both, preferred_element_type=F32)

    @pl.when(pl.program_id(0) == pl.num_programs(0) - 1)
    def _():
        for j in range(BLOCKS):
            out_ref[j] = acc[at_ref[j]].astype(BF16)


def packed_up(at, x, up_weight, bias, pos, part):
    clusters, width, neurons = up_weight.shape
    tokens = x.shape[0]
    return pl.pallas_call(
        up_kernel,
        grid_spec=pltpu.PrefetchScalarGridSpec(
            num_scalar_prefetch=1,
            grid=(clusters // PACK,),
            in_specs=[
                pl.BlockSpec((tokens, width), lambda i, at: (0, 0)),
                pl.BlockSpec((PACK, width, neurons), lambda i, at: (i, 0, 0)),
                pl.BlockSpec((1, PACK, neurons), lambda i, at: (i, 0, 0)),
                pl.BlockSpec((1, BLOCKS, PACK * tokens // BLOCKS), lambda i, at: (i, part, 0)),
            ],
            out_specs=pl.BlockSpec((BLOCKS, SLOTS, neurons), lambda i, at: (0, 0, 0)),
            scratch_shapes=[pltpu.VMEM((BLOCKS, SLOTS, neurons), F32)],
        ),
        out_shape=jax.ShapeDtypeStruct((BLOCKS, SLOTS, neurons), BF16),
        compiler_params=pltpu.CompilerParams(vmem_limit_bytes=VMEM),
        cost_estimate=pl.CostEstimate(
            flops=4 * tokens * width * clusters * neurons, bytes_accessed=9 << 20, transcendentals=0
        ),
    )(at, x, up_weight, bias, pos)


def down_kernel(at_ref, packed_ref, pos_ref, w_ref, out_ref, hidden):
    neurons = packed_ref.shape[-1]
    span = hidden.shape[0] // BLOCKS

    @pl.when(pl.program_id(0) == 0)
    def _():
        slot = lax.broadcasted_iota(I32, (SLOTS, PACK * span), 0)
        for j in range(BLOCKS):
            b = at_ref[j]
            to = pl.ds(pl.multiple_of(b * span, span), span)
            for q in range(pos_ref.shape[0]):
                take = jnp.where(slot == pos_ref[q, pl.ds(b, 1), :], 1.0, 0.0).astype(BF16)
                both = lax.dot_general(
                    take, packed_ref[j], (((0,), (0,)), ((), ())), preferred_element_type=F32
                ).astype(BF16)
                for k in range(PACK):
                    c = q * PACK + k
                    hidden[to, c * neurons : (c + 1) * neurons] = both[k * span : (k + 1) * span]

    wide = w_ref[...].reshape(-1, w_ref.shape[-1])
    out_ref[...] = jnp.dot(hidden[...], wide, preferred_element_type=F32).astype(BF16)


def packed_down(at, packed, pos, down_weight, tokens, part):
    clusters, neurons, width = down_weight.shape
    return pl.pallas_call(
        down_kernel,
        grid_spec=pltpu.PrefetchScalarGridSpec(
            num_scalar_prefetch=1,
            grid=(width // TILE,),
            in_specs=[
                pl.BlockSpec((BLOCKS, SLOTS, neurons), lambda n, at: (0, part, 0)),
                pl.BlockSpec((pos.shape[0], BLOCKS, pos.shape[2]), lambda n, at: (0, part, 0)),
                pl.BlockSpec((clusters, neurons, TILE), lambda n, at: (0, 0, n)),
            ],
            out_specs=pl.BlockSpec((tokens, TILE), lambda n, at: (0, n)),
            scratch_shapes=[pltpu.VMEM((tokens, clusters * neurons), BF16)],
        ),
        out_shape=jax.ShapeDtypeStruct((tokens, width), BF16),
        compiler_params=pltpu.CompilerParams(vmem_limit_bytes=VMEM),
        cost_estimate=pl.CostEstimate(
            flops=2 * tokens * clusters * neurons * width, bytes_accessed=7 << 20, transcendentals=0
        ),
    )(at, packed, pos, down_weight)


def slots_of(mask):
    clusters, _, span = mask.shape
    hits = mask.astype(BF16)
    before = jnp.triu(jnp.ones((span, span), BF16), 1)
    ahead = jnp.triu(jnp.ones((clusters, clusters), BF16), 1)
    each = jnp.sum(hits.astype(F32), axis=0).astype(BF16)
    base = jnp.dot(each, before, preferred_element_type=F32)
    within = jnp.einsum("kbt,kc->cbt", hits, ahead, preferred_element_type=F32)
    return jnp.where(mask, base[None] + within, -1.0).astype(I32)


def loop_spread(block, axes):
    n, me = lax.axis_size(axes), lax.axis_index(axes)

    def step(k, held):
        block, found = held
        block = from_peer(block, axes, 1)
        return block, lax.dynamic_update_index_in_dim(found, block, (me + k) % n, 0)

    found = lax.dynamic_update_index_in_dim(jnp.zeros((n,) + block.shape, block.dtype), block, me, 0)
    return lax.fori_loop(1, n, step, (block, found))[1]


def loop_total(blocks, axes):
    n, me = lax.axis_size(axes), lax.axis_index(axes)

    def step(k, sum):
        sum = from_peer(sum, axes, 1)
        return sum + lax.dynamic_index_in_dim(blocks, (me + k) % n, 0, False).astype(F32)

    first = lax.dynamic_index_in_dim(blocks, (me + 1) % n, 0, False).astype(F32)
    return lax.fori_loop(2, n + 1, step, first)


def dense(activations, picks, up_weight, up_bias, down_weight):
    rows, width = activations.shape
    clusters, _, neurons = up_weight.shape
    tokens, span = picks.shape[0], picks.shape[0] // BLOCKS
    dp, clus = ("x", "core"), ("z", "y")
    x = loop_spread(activations, clus).reshape(tokens, width)
    picked = lax.dynamic_slice_in_dim(picks, lax.axis_index(dp) * span, span, 0)

    def cluster(c, out):
        part = jnp.dot(x, up_weight[c], preferred_element_type=F32)
        summed = loop_total(part.reshape(BLOCKS, span, neurons), dp) + up_bias[c]
        keep = jnp.any(picked == lax.axis_index(clus) * clusters + c, axis=1, keepdims=True)
        hidden = jnp.where(keep, jnp.maximum(summed, 0.0), 0.0).astype(BF16)
        hidden = loop_spread(hidden, dp).reshape(tokens, neurons)
        return out + jnp.dot(hidden, down_weight[c], preferred_element_type=F32)

    out = lax.fori_loop(0, clusters, cluster, jnp.zeros((tokens, width), F32)).astype(BF16)
    return loop_total(out.reshape(-1, rows, width), clus).astype(BF16)


def on_device(activations, picks, up_weight, up_bias, down_weight):
    rows, width = activations.shape
    clusters, _, neurons = up_weight.shape
    cut = rows // 2
    tokens = NZ * NY * cut
    span = tokens // BLOCKS
    core, xi = lax.axis_index("core"), lax.axis_index("x")
    zi, yi = lax.axis_index("z"), lax.axis_index("y")

    first, second = activations[:cut], activations[cut:]
    first = spread(first, "z")

    wanted = (zi * NY + yi) * clusters + jnp.arange(clusters, dtype=I32)
    mask = jnp.any(picks.T[None, :, :] == wanted[:, None, None], axis=1)
    mask = mask.reshape(clusters, NZ, NY, 2, cut)
    mask_1 = mask[:, :, :, 0].transpose(0, 2, 1, 3).reshape(clusters, BLOCKS, span)
    mask_2 = jnp.roll(mask[:, :, :, 1], (-zi, -yi), axis=(1, 2)).reshape(clusters, BLOCKS, span)
    pos = slots_of(jnp.concatenate([mask_1, mask_2], axis=1))
    pos = pos.reshape(clusters // PACK, PACK, 2 * BLOCKS, span).transpose(0, 2, 1, 3)
    pos = pos.reshape(clusters // PACK, 2 * BLOCKS, PACK * span)

    second, pos = lax.optimization_barrier((second, pos))
    near = jnp.stack([second] + [from_peer(second, "y", k) for k in range(1, NY)])
    near, first = lax.optimization_barrier((near, first))
    x_1 = spread(first, "y").reshape(tokens, width)
    x_2, x_1 = ring_spread(near, "z", x_1)
    x_2 = x_2.reshape(tokens, width)

    groups = picks.T // clusters
    named = jnp.sum(
        (groups[None] == jnp.arange(NZ * NY, dtype=I32)[:, None, None]).astype(F32), axis=1
    ).astype(BF16)
    token = jnp.arange(2 * tokens, dtype=I32)
    z, y, part = token // (2 * cut * NY), token // (2 * cut) % NY, token // cut % 2
    block = jnp.where(part == 0, (y * NZ + z) * BLOCKS // (NY * NZ), BLOCKS + z * BLOCKS // NZ)
    belongs = (block[:, None] == jnp.arange(2 * BLOCKS, dtype=I32)[None]).astype(BF16)
    fits = jnp.max(jnp.dot(named, belongs, preferred_element_type=F32)) <= SLOTS

    order = [((core + j // NX) % NC) * NX + (xi + j % NX) % NX for j in range(BLOCKS)]
    at = jnp.stack(order).astype(I32)
    bias = (up_bias * (1.0 / BLOCKS)).reshape(clusters // PACK, PACK, neurons)

    def pair_of(x, part):
        rows = packed_up(at, x, up_weight, bias, pos, part)
        return rows[:NX].astype(F32) + from_peer(rows[NX:], "core", 1).astype(F32)

    def sum_of(rows):
        summed = rows[0]
        rows = rows.astype(BF16)
        for k in range(1, NX):
            summed = summed + from_peer(rows[k], "x", -k).astype(F32)
        return jnp.maximum(summed, 0.0).astype(BF16)

    def all_of(own):
        own = jnp.stack([own] + [from_peer(own, "x", k) for k in range(1, NX)])
        return jnp.concatenate([own, from_peer(own, "core", 1)], axis=0)

    rows_1, rows_2 = pair_of(x_1, 0), pair_of(x_2, 1)
    packed = all_of(sum_of(jnp.concatenate([rows_1, rows_2], axis=1)))
    out_1 = packed_down(at, packed, pos, down_weight, tokens, 0).reshape(NY, NZ, cut, width)
    out_2 = packed_down(at, packed, pos, down_weight, tokens, 1).reshape(NZ, NY, cut, width)
    out_1 = total(exchange(out_1, "y")).astype(BF16)
    out_2, out_1 = ring_total(out_2, "z", out_1)
    out_1 = total(exchange(out_1, "z")).astype(BF16)
    out_2 = out_2.astype(BF16)
    done = out_2[0].astype(F32)
    for k in range(1, NY):
        done = done + from_peer(out_2[k], "y", -k).astype(F32)
    out = jnp.concatenate([out_1, done.astype(BF16)], axis=0)
    whole = (activations, picks, up_weight, up_bias, down_weight)
    return lax.cond(fits, lambda: out, lambda: dense(*whole))


def solution(mesh):
    grid = Mesh(mesh.devices.reshape(NX, NC, NZ, NY), ("x", "core", "z", "y"))
    dp, clus = ("x", "core"), ("z", "y")
    placed = (P(clus, dp), P(), P(clus, dp, None), P(clus, None), P(clus, None, dp))
    return jax.shard_map(
        on_device, mesh=grid, in_specs=placed, out_specs=P(clus, dp), check_vma=False
    )
```

```python
import jax
import jax.numpy as jnp
from jax import lax
from jax.experimental import pallas as pl
from jax.experimental.pallas import tpu as pltpu
from jax.sharding import Mesh
from jax.sharding import PartitionSpec as P

F32, BF16, I32 = jnp.float32, jnp.bfloat16, jnp.int32
NX, NC, NZ, NY = 4, 2, 8, 4
BLOCKS = NX * NC
SLOTS = 192
PACK = 4
TILE = 512
VMEM = 32 << 20


def spread(block, axis):
    peers = lax.axis_size(axis)
    return lax.all_to_all(
        jnp.broadcast_to(block[None], (peers,) + block.shape), axis, split_axis=0, concat_axis=0
    )


def exchange(blocks, axis):
    return lax.all_to_all(blocks, axis, split_axis=0, concat_axis=0)


def total(blocks):
    return jnp.sum(blocks.astype(F32), axis=0)


def from_peer(block, axis, step):
    n = lax.axis_size(axis)
    return lax.ppermute(block, axis, [((i + step) % n, i) for i in range(n)])


def ring_spread(block, axis, beside):
    n = lax.axis_size(axis)
    found = {0: block}
    for k in range(1, n // 2):
        found[k] = from_peer(found[k - 1], axis, 1)
        found[n - k] = from_peer(found[(n + 1 - k) % n], axis, -1)
    last, beside = lax.optimization_barrier((found[n // 2 - 1], beside))
    found[n // 2] = from_peer(last, axis, 1)
    return [found[k] for k in range(n)], beside


def ring_total(blocks, axis):
    n = blocks.shape[0]
    down, up = blocks[n // 2], blocks[n // 2 - 1]
    for k in range(n // 2 - 1, 0, -1):
        down = (blocks[n - k] + from_peer(down, axis, 1).astype(F32)).astype(BF16)
        if k < n // 2 - 1:
            up = (blocks[k] + from_peer(up, axis, -1).astype(F32)).astype(BF16)
    return blocks[0] + from_peer(down, axis, 1).astype(F32) + from_peer(up, axis, -1).astype(F32)


def up_kernel(at_ref, *refs):
    *pieces, w_ref, bias_ref, pos_ref, out_ref, acc, x_ref = refs
    span, neurons = x_ref.shape[0] // BLOCKS, w_ref.shape[-1]
    slot = lax.broadcasted_iota(I32, (SLOTS, PACK * span), 0)

    @pl.when(pl.program_id(0) == 0)
    def _():
        acc[...] = jnp.zeros_like(acc)
        rows = x_ref.shape[0] // len(pieces)
        for k, piece in enumerate(pieces):
            x_ref[k * rows : (k + 1) * rows] = piece[...]

    pairs = []
    for p in range(0, PACK, 2):
        wide = jnp.concatenate([w_ref[p], w_ref[p + 1]], axis=1)
        bias = jnp.concatenate([bias_ref[0, p : p + 1], bias_ref[0, p + 1 : p + 2]], axis=1)
        pre = jnp.dot(x_ref[...], wide, preferred_element_type=F32)
        pairs.append((pre + bias).astype(BF16))
    for b in range(BLOCKS):
        rows = slice(b * span, (b + 1) * span)
        both = jnp.concatenate(
            [p[rows, k * neurons : (k + 1) * neurons] for p in pairs for k in range(2)], axis=0
        )
        take = jnp.where(slot == pos_ref[0, b : b + 1, :], 1.0, 0.0).astype(BF16)
        acc[b] += jnp.dot(take, both, preferred_element_type=F32)

    @pl.when(pl.program_id(0) == pl.num_programs(0) - 1)
    def _():
        for j in range(BLOCKS):
            out_ref[j] = acc[at_ref[j]].astype(BF16)


def packed_up(at, pieces, up_weight, bias, pos, part):
    clusters, width, neurons = up_weight.shape
    rows = pieces[0].shape[0]
    tokens = rows * len(pieces)
    return pl.pallas_call(
        up_kernel,
        grid_spec=pltpu.PrefetchScalarGridSpec(
            num_scalar_prefetch=1,
            grid=(clusters // PACK,),
            in_specs=[
                *[pl.BlockSpec((rows, width), lambda i, at: (0, 0)) for _ in pieces],
                pl.BlockSpec((PACK, width, neurons), lambda i, at: (i, 0, 0)),
                pl.BlockSpec((1, PACK, neurons), lambda i, at: (i, 0, 0)),
                pl.BlockSpec((1, BLOCKS, PACK * tokens // BLOCKS), lambda i, at: (i, part, 0)),
            ],
            out_specs=pl.BlockSpec((BLOCKS, SLOTS, neurons), lambda i, at: (0, 0, 0)),
            scratch_shapes=[
                pltpu.VMEM((BLOCKS, SLOTS, neurons), F32),
                pltpu.VMEM((tokens, width), BF16),
            ],
        ),
        out_shape=jax.ShapeDtypeStruct((BLOCKS, SLOTS, neurons), BF16),
        compiler_params=pltpu.CompilerParams(vmem_limit_bytes=VMEM),
        cost_estimate=pl.CostEstimate(
            flops=4 * tokens * width * clusters * neurons, bytes_accessed=9 << 20, transcendentals=0
        ),
    )(at, *pieces, up_weight, bias, pos)


def down_kernel(at_ref, packed_ref, pos_ref, w_ref, out_ref, hidden):
    neurons = packed_ref.shape[-1]
    span = hidden.shape[0] // BLOCKS

    @pl.when(pl.program_id(0) == 0)
    def _():
        slot = lax.broadcasted_iota(I32, (SLOTS, PACK * span), 0)
        for j in range(BLOCKS):
            b = at_ref[j]
            to = pl.ds(pl.multiple_of(b * span, span), span)
            for q in range(pos_ref.shape[0]):
                take = jnp.where(slot == pos_ref[q, pl.ds(b, 1), :], 1.0, 0.0).astype(BF16)
                both = lax.dot_general(
                    take, packed_ref[j], (((0,), (0,)), ((), ())), preferred_element_type=F32
                ).astype(BF16)
                for k in range(PACK):
                    c = q * PACK + k
                    hidden[to, c * neurons : (c + 1) * neurons] = both[k * span : (k + 1) * span]

    wide = w_ref[...].reshape(-1, w_ref.shape[-1])
    out_ref[...] = jnp.dot(hidden[...], wide, preferred_element_type=F32).astype(BF16)


def packed_down(at, packed, pos, down_weight, tokens, part):
    clusters, neurons, width = down_weight.shape
    return pl.pallas_call(
        down_kernel,
        grid_spec=pltpu.PrefetchScalarGridSpec(
            num_scalar_prefetch=1,
            grid=(width // TILE,),
            in_specs=[
                pl.BlockSpec((BLOCKS, SLOTS, neurons), lambda n, at: (0, part, 0)),
                pl.BlockSpec((pos.shape[0], BLOCKS, pos.shape[2]), lambda n, at: (0, part, 0)),
                pl.BlockSpec((clusters, neurons, TILE), lambda n, at: (0, 0, n)),
            ],
            out_specs=pl.BlockSpec((tokens, TILE), lambda n, at: (0, n)),
            scratch_shapes=[pltpu.VMEM((tokens, clusters * neurons), BF16)],
        ),
        out_shape=jax.ShapeDtypeStruct((tokens, width), BF16),
        compiler_params=pltpu.CompilerParams(vmem_limit_bytes=VMEM),
        cost_estimate=pl.CostEstimate(
            flops=2 * tokens * clusters * neurons * width, bytes_accessed=7 << 20, transcendentals=0
        ),
    )(at, packed, pos, down_weight)


def slots_of(mask):
    clusters, _, span = mask.shape
    hits = mask.astype(BF16)
    before = jnp.triu(jnp.ones((span, span), BF16), 1)
    ahead = jnp.triu(jnp.ones((clusters, clusters), BF16), 1)
    each = jnp.sum(hits.astype(F32), axis=0).astype(BF16)
    base = jnp.dot(each, before, preferred_element_type=F32)
    within = jnp.einsum("kbt,kc->cbt", hits, ahead, preferred_element_type=F32)
    return jnp.where(mask, base[None] + within, -1.0).astype(I32)


def loop_spread(block, axes):
    n, me = lax.axis_size(axes), lax.axis_index(axes)

    def step(k, held):
        block, found = held
        block = from_peer(block, axes, 1)
        return block, lax.dynamic_update_index_in_dim(found, block, (me + k) % n, 0)

    found = lax.dynamic_update_index_in_dim(jnp.zeros((n,) + block.shape, block.dtype), block, me, 0)
    return lax.fori_loop(1, n, step, (block, found))[1]


def loop_total(blocks, axes):
    n, me = lax.axis_size(axes), lax.axis_index(axes)

    def step(k, sum):
        sum = from_peer(sum, axes, 1)
        return sum + lax.dynamic_index_in_dim(blocks, (me + k) % n, 0, False).astype(F32)

    first = lax.dynamic_index_in_dim(blocks, (me + 1) % n, 0, False).astype(F32)
    return lax.fori_loop(2, n + 1, step, first)


def dense(activations, picks, up_weight, up_bias, down_weight):
    rows, width = activations.shape
    clusters, _, neurons = up_weight.shape
    tokens, span = picks.shape[0], picks.shape[0] // BLOCKS
    dp, clus = ("x", "core"), ("z", "y")
    x = loop_spread(activations, clus).reshape(tokens, width)
    picked = lax.dynamic_slice_in_dim(picks, lax.axis_index(dp) * span, span, 0)

    def cluster(c, out):
        part = jnp.dot(x, up_weight[c], preferred_element_type=F32)
        summed = loop_total(part.reshape(BLOCKS, span, neurons), dp) + up_bias[c]
        keep = jnp.any(picked == lax.axis_index(clus) * clusters + c, axis=1, keepdims=True)
        hidden = jnp.where(keep, jnp.maximum(summed, 0.0), 0.0).astype(BF16)
        hidden = loop_spread(hidden, dp).reshape(tokens, neurons)
        return out + jnp.dot(hidden, down_weight[c], preferred_element_type=F32)

    out = lax.fori_loop(0, clusters, cluster, jnp.zeros((tokens, width), F32)).astype(BF16)
    return loop_total(out.reshape(-1, rows, width), clus).astype(BF16)


def on_device(activations, picks, up_weight, up_bias, down_weight):
    rows, width = activations.shape
    clusters, _, neurons = up_weight.shape
    cut = rows // 2
    tokens = NZ * NY * cut
    span = tokens // BLOCKS
    core, xi = lax.axis_index("core"), lax.axis_index("x")
    zi, yi = lax.axis_index("z"), lax.axis_index("y")

    first, second = activations[:cut], activations[cut:]
    first = spread(first, "z")

    wanted = (zi * NY + yi) * clusters + jnp.arange(clusters, dtype=I32)
    mask = jnp.any(picks.T[None, :, :] == wanted[:, None, None], axis=1)
    mask = mask.reshape(clusters, NZ, NY, 2, cut)
    mask_1 = mask[:, :, :, 0].transpose(0, 2, 1, 3).reshape(clusters, BLOCKS, span)
    mask_2 = jnp.roll(mask[:, :, :, 1], (-zi, -yi), axis=(1, 2)).reshape(clusters, BLOCKS, span)
    pos = slots_of(jnp.concatenate([mask_1, mask_2], axis=1))
    pos = pos.reshape(clusters // PACK, PACK, 2 * BLOCKS, span).transpose(0, 2, 1, 3)
    pos = pos.reshape(clusters // PACK, 2 * BLOCKS, PACK * span)

    second, pos = lax.optimization_barrier((second, pos))
    near = jnp.stack([second] + [from_peer(second, "y", k) for k in range(1, NY)])
    near, first = lax.optimization_barrier((near, first))
    x_1 = spread(first, "y").reshape(tokens, width)
    x_2, x_1 = ring_spread(near, "z", x_1)
    x_2 = [x.reshape(tokens // NZ, width) for x in x_2]

    groups = picks.T // clusters
    named = jnp.sum(
        (groups[None] == jnp.arange(NZ * NY, dtype=I32)[:, None, None]).astype(F32), axis=1
    ).astype(BF16)
    token = jnp.arange(2 * tokens, dtype=I32)
    z, y, part = token // (2 * cut * NY), token // (2 * cut) % NY, token // cut % 2
    block = jnp.where(part == 0, (y * NZ + z) * BLOCKS // (NY * NZ), BLOCKS + z * BLOCKS // NZ)
    belongs = (block[:, None] == jnp.arange(2 * BLOCKS, dtype=I32)[None]).astype(BF16)
    fits = jnp.max(jnp.dot(named, belongs, preferred_element_type=F32)) <= SLOTS

    order = [((core + j // NX) % NC) * NX + (xi + j % NX) % NX for j in range(BLOCKS)]
    at = jnp.stack(order).astype(I32)
    bias = (up_bias * (1.0 / BLOCKS)).reshape(clusters // PACK, PACK, neurons)

    def pair_of(x, part):
        rows = packed_up(at, x, up_weight, bias, pos, part)
        return rows[:NX].astype(F32) + from_peer(rows[NX:], "core", 1).astype(F32)

    def sum_of(rows):
        summed = rows[0]
        rows = rows.astype(BF16)
        for k in range(1, NX):
            summed = summed + from_peer(rows[k], "x", -k).astype(F32)
        return jnp.maximum(summed, 0.0).astype(BF16)

    def all_of(own):
        own = jnp.stack([own] + [from_peer(own, "x", k) for k in range(1, NX)])
        return jnp.concatenate([own, from_peer(own, "core", 1)], axis=0)

    rows_1, rows_2 = pair_of([x_1], 0), pair_of(x_2, 1)
    packed = all_of(sum_of(jnp.concatenate([rows_1, rows_2], axis=1)))
    out_1 = packed_down(at, packed, pos, down_weight, tokens, 0).reshape(NY, NZ, cut, width)
    out_2 = packed_down(at, packed, pos, down_weight, tokens, 1).reshape(NZ, NY, cut, width)
    out_1 = total(exchange(out_1, "y")).astype(BF16)
    out_2 = ring_total(out_2, "z").astype(BF16)
    out_1 = total(exchange(out_1, "z")).astype(BF16)
    done = out_2[0].astype(F32)
    for k in range(1, NY):
        done = done + from_peer(out_2[k], "y", -k).astype(F32)
    out = jnp.concatenate([out_1, done.astype(BF16)], axis=0)
    whole = (activations, picks, up_weight, up_bias, down_weight)
    return lax.cond(fits, lambda: out, lambda: dense(*whole))


def solution(mesh):
    grid = Mesh(mesh.devices.reshape(NX, NC, NZ, NY), ("x", "core", "z", "y"))
    dp, clus = ("x", "core"), ("z", "y")
    placed = (P(clus, dp), P(), P(clus, dp, None), P(clus, None), P(clus, None, dp))
    return jax.shard_map(
        on_device, mesh=grid, in_specs=placed, out_specs=P(clus, dp), check_vma=False
    )
```
